256 devices in a mesh: shard: 64 (over z, y_hi, x), heads: 2 (over y_lo), tensor: 2 (over core).
Axes of the slice: x: 4, y: 4 (y_hi: 2, y_lo: 2; y = y_hi * 2 + y_lo), z: 8, core: 2. Of those that a mesh axis runs over, the one named last changes fastest.
Arguments:
- noisy_patches: bfloat16 [256, 4096], P('shard'), may hold values from -6 to 6
- true_noise: bfloat16 [256, 4096], P('shard'), may hold values from -10 to 10
- timesteps: int32 [256], P('shard'), may hold values from 0 to 999
- labels: int32 [256], P('shard'), may hold values from 0 to 999
- attn_w: float32 [4, 1024, 1024], P(None, 'shard', 'heads'), may hold values from -2 to 2
- attn_mom: float32 [4, 1024, 1024], P(None, 'shard', 'heads'), may hold values from -1.1444092e-05 to 1.1444092e-05
- mlp_w: float32 [8, 1024, 1024], P(None, 'shard', 'tensor'), may hold values from -2 to 2
- mlp_mom: float32 [8, 1024, 1024], P(None, 'shard', 'tensor'), may hold values from -1.1444092e-05 to 1.1444092e-05
- mod_w: float32 [8, 1024, 1024], P(None, 'shard'), may hold values from -0.1875 to 0.1875
- mod_mom: float32 [8, 1024, 1024], P(None, 'shard'), may hold values from -1.1444092e-05 to 1.1444092e-05
- temb_w: float32 [1024, 1280], P('shard'), may hold values from -2 to 2
- temb_mom: float32 [1024, 1280], P('shard'), may hold values from -1.1444092e-05 to 1.1444092e-05
- label_table: float32 [1000, 1024], P(None, ('shard', 'heads', 'tensor')), may hold values from -6 to 6
- table_first: float32 [1000, 1024], P(None, ('shard', 'heads', 'tensor')), may hold values from -5.9604645e-07 to 5.9604645e-07
- table_second: float32 [1000, 1024], P(None, ('shard', 'heads', 'tensor')), may hold values from 9.536743e-15 to 3.8146972e-14
- io_w: float32 [2, 16, 1024], P(None, None, ('shard', 'heads', 'tensor')), may hold values from -2 to 2
- io_first: float32 [2, 16, 1024], P(None, None, ('shard', 'heads', 'tensor')), may hold values from -4.5776367e-05 to 4.5776367e-05
- io_second: float32 [2, 16, 1024], P(None, None, ('shard', 'heads', 'tensor')), may hold values from 6.1035156e-11 to 2.4414062e-10
- vec_w: float32 [19, 1024], P(None, ('shard', 'heads', 'tensor')), may hold values from -1.25 to 1.25
- vec_first: float32 [19, 1024], P(None, ('shard', 'heads', 'tensor')), may hold values from -4.5776367e-05 to 4.5776367e-05
- vec_second: float32 [19, 1024], P(None, ('shard', 'heads', 'tensor')), may hold values from 6.1035156e-11 to 2.4414062e-10
- head_b: float32 [16], replicated, may hold values from -1.25 to 1.25
- headb_first: float32 [16], replicated, may hold values from -0.00012207031 to 0.00012207031
- headb_second: float32 [16], replicated, may hold values from 3.8146972e-10 to 1.5258789e-09
Outputs:
- loss: float32 [], replicated
- grad_norm: float32 [], replicated
- attn_new: float32 [4, 1024, 1024], P(None, 'shard', 'heads')
- attn_moment: float32 [4, 1024, 1024], P(None, 'shard', 'heads')
- attn_copy: bfloat16 [4, 1024, 1024], P(None, 'shard', 'heads')
- mlp_new: float32 [8, 1024, 1024], P(None, 'shard', 'tensor')
- mlp_moment: float32 [8, 1024, 1024], P(None, 'shard', 'tensor')
- mlp_copy: bfloat16 [8, 1024, 1024], P(None, 'shard', 'tensor')
- mod_new: float32 [8, 1024, 1024], P(None, 'shard')
- mod_moment: float32 [8, 1024, 1024], P(None, 'shard')
- mod_copy: bfloat16 [8, 1024, 1024], P(None, 'shard')
- temb_new: float32 [1024, 1280], P('shard')
- temb_moment: float32 [1024, 1280], P('shard')
- table_new: float32 [1000, 1024], P(None, ('shard', 'heads', 'tensor'))
- table_first_new: float32 [1000, 1024], P(None, ('shard', 'heads', 'tensor'))
- table_second_new: float32 [1000, 1024], P(None, ('shard', 'heads', 'tensor'))
- table_copy: bfloat16 [1000, 1024], P(None, ('shard', 'heads', 'tensor'))
- io_new: float32 [2, 16, 1024], P(None, None, ('shard', 'heads', 'tensor'))
- io_first_new: float32 [2, 16, 1024], P(None, None, ('shard', 'heads', 'tensor'))
- io_second_new: float32 [2, 16, 1024], P(None, None, ('shard', 'heads', 'tensor'))
- vec_new: float32 [19, 1024], P(None, ('shard', 'heads', 'tensor'))
- vec_first_new: float32 [19, 1024], P(None, ('shard', 'heads', 'tensor'))
- vec_second_new: float32 [19, 1024], P(None, ('shard', 'heads', 'tensor'))
- headb_new: float32 [16], replicated
- headb_first_new: float32 [16], replicated
- headb_second_new: float32 [16], replicated
The draws below stay inside these ranges and needn't reach their ends.
All inputs are finite; a program needn't handle non-finite values.
Results may differ from the reference program's by a relative error of at most 0.0091.
Values may be sent and summed in bfloat16 or wider, within the bound.
No kernel may reach another device: no remote copies, remote signals or barrier semaphores. Data moves between devices by JAX's collectives and lax.ppermute only.
A program may use at most 320 MiB of HBM per device.

```python
import math
import jax
import jax.numpy as jnp
from jax import lax

D = 1024
HEADS = 16
HDIM = 64
FF = 4096
FREQ = 256
NCLS = 1000
PATCH = 16
GRID = 16
SEQ = 256
LATENTS = 256
RB = 16
NS_STEPS = 5
STEP = 10
VROWS = 19
COUNT = 1048576


def column_factor(total_cols, col_ratio):
    places = jnp.arange(total_cols, dtype=jnp.float32) / max(total_cols - 1, 1)
    return jnp.exp(math.log(col_ratio) * (places - 0.5))


def draw_true_noise(key, part):
    key = jax.random.fold_in(key, 11)
    dims_all = (LATENTS, SEQ * PATCH)
    places = jnp.arange(LATENTS, dtype=jnp.float32)[:, None] / (LATENTS - 1)
    base_draw = jnp.clip(jax.random.normal(key, dims_all, jnp.float32), -4.0, 4.0)
    return (base_draw * (1.0 + 1.5 * places)).astype(jnp.bfloat16)


def draw_attn_w(key, part):
    key = jax.random.fold_in(key, 12)
    dims_all = (4, D, D)
    base_draw = jnp.clip(jax.random.normal(key, dims_all, jnp.float32), -4.0, 4.0)
    col_ratio = 1.7320508
    slot_scale = jnp.array([1.0, 1.0, 1.0, 4.0], jnp.float32)[:, None, None]
    return base_draw * column_factor(D, col_ratio) * slot_scale / math.sqrt(D)


def draw_mlp_w(key, part):
    key = jax.random.fold_in(key, 13)
    fc_blocks = FF // D
    dims_all = (2 * fc_blocks, D, D)
    base_draw = jnp.clip(jax.random.normal(key, dims_all, jnp.float32), -4.0, 4.0)
    col_ratio = 1.7320508
    slot_scale = jnp.where(jnp.arange(2 * fc_blocks) < fc_blocks, 1.0 / math.sqrt(D), 2.0 / math.sqrt(FF))
    return base_draw * column_factor(D, col_ratio) * slot_scale[:, None, None]


def draw_temb_w(key, part):
    key = jax.random.fold_in(key, 14)
    dims_all = (D, FREQ + D)
    base_draw = jnp.clip(jax.random.normal(key, dims_all, jnp.float32), -4.0, 4.0)
    col_scale = jnp.where(jnp.arange(FREQ + D) < FREQ, 1.0 / math.sqrt(FREQ), 1.0 / math.sqrt(D))
    return base_draw * col_scale[None, :]


def draw_io_w(key, part):
    key = jax.random.fold_in(key, 15)
    dims_all = (2, PATCH, D)
    base_draw = jnp.clip(jax.random.normal(key, dims_all, jnp.float32), -4.0, 4.0)
    col_ratio = 1.7320508
    slot_scale = jnp.array([1.0 / math.sqrt(PATCH), 1.0 / math.sqrt(D)], jnp.float32)[:, None, None]
    return base_draw * column_factor(D, col_ratio) * slot_scale


def with_ends(values, key, smallest, high):
    longest = values.shape.index(max(values.shape))
    spots = []
    for shift in (0, 1):
        where = [jax.random.randint(jax.random.fold_in(key, axis), (), 0, length) for axis, length in enumerate(values.shape)]
        where[longest] = (where[longest] + shift) % values.shape[longest]
        spots.append(tuple(where))
    return values.at[spots[0]].set(smallest).at[spots[1]].set(high)


def steps_of(key, shape, cuts, least, largest):
    gain = 1.0
    for axis_at, parts in cuts:
        steps = jax.random.uniform(jax.random.fold_in(jax.random.fold_in(key, 6), axis_at), (parts,), jnp.float32, least / len(cuts), largest / len(cuts))
        gain = gain * jnp.repeat(jnp.exp(steps), shape[axis_at] // parts).reshape((-1,) + (1,) * (len(shape) - 1 - axis_at))
    return gain


def gaussian(key, extent, spread, bound, shards=(), held_as=jnp.bfloat16):
    result = jax.random.normal(key, extent, jnp.float32) * spread
    if len(shards) > 0:
        result = steps_of(key, extent, shards, -0.22, 0.18) * result
    return jnp.clip(result, min=-bound, max=bound).astype(held_as)


def setup_inputs(seed: int = 0) -> dict:
    arg_keys = jax.random.split(jax.random.key(seed), 25)
    noisy_patches = gaussian(arg_keys[0], (LATENTS, SEQ * PATCH), 1.0, 6.0, ((0, 64),))
    true_noise = draw_true_noise(jax.random.fold_in(arg_keys[24], 71), 0)
    timesteps = with_ends(jax.random.randint(arg_keys[2], (LATENTS,), 0, 1000), jax.random.fold_in(arg_keys[2], 1), 0, 999).astype(jnp.int32)
    labels = with_ends(jax.random.randint(arg_keys[3], (LATENTS,), 0, NCLS), jax.random.fold_in(arg_keys[3], 1), 0, NCLS - 1).astype(jnp.int32)
    attn_w = draw_attn_w(jax.random.fold_in(arg_keys[24], 71), 0)
    attn_mom = gaussian(arg_keys[5], (4, D, D), (0.002 / D), 1.1444091796875e-05, ((1, 64), (2, 2)), jnp.float32)
    mlp_w = draw_mlp_w(jax.random.fold_in(arg_keys[24], 71), 0)
    mlp_mom = gaussian(arg_keys[7], (2 * FF // D, D, D), (0.002 / D), 1.1444091796875e-05, ((1, 64), (2, 2)), jnp.float32)
    mod_w = gaussian(arg_keys[8], (8, D, D), D ** -0.5, 0.1875, ((1, 64),), jnp.float32)
    mod_mom = gaussian(arg_keys[9], (8, D, D), (0.002 / D), 1.1444091796875e-05, ((1, 64),), jnp.float32)
    temb_w = draw_temb_w(jax.random.fold_in(arg_keys[24], 71), 0)
    temb_mom = gaussian(arg_keys[11], (D, FREQ + D), (0.002 / D), 1.1444091796875e-05, ((0, 64),), jnp.float32)
    label_table = gaussian(arg_keys[12], (NCLS, D), 1.0, 6.0, ((1, 256),), jnp.float32)
    table_first = gaussian(arg_keys[13], (NCLS, D), (0.0001 / D), 5.960464477539062e-07, ((1, 256),), jnp.float32)
    table_second = jnp.clip(jnp.exp(math.log(3.814697242441288e-14) - 1.3862944 * jax.random.uniform(arg_keys[14], (NCLS, D), jnp.float32) ** steps_of(arg_keys[14], (NCLS, D), ((1, 256),), -0.2, 0.2)), 9.53674310610322e-15, 3.814697242441288e-14)
    io_w = draw_io_w(jax.random.fold_in(arg_keys[24], 71), 0)
    io_first = gaussian(arg_keys[16], (2, PATCH, D), (0.008 / D), 4.57763671875e-05, ((2, 256),), jnp.float32)
    io_second = jnp.clip(jnp.exp(math.log(2.441406243836042e-10) - 1.3862944 * jax.random.uniform(arg_keys[17], (2, PATCH, D), jnp.float32) ** steps_of(arg_keys[17], (2, PATCH, D), ((2, 256),), -0.2, 0.2)), 6.103515609590104e-11, 2.441406243836042e-10)
    vec_w = gaussian(arg_keys[18], (VROWS, D), 0.2, 1.25, ((1, 256),), jnp.float32)
    vec_first = gaussian(arg_keys[19], (VROWS, D), (0.008 / D), 4.57763671875e-05, ((1, 256),), jnp.float32)
    vec_second = jnp.clip(jnp.exp(math.log(2.441406243836042e-10) - 1.3862944 * jax.random.uniform(arg_keys[20], (VROWS, D), jnp.float32) ** steps_of(arg_keys[20], (VROWS, D), ((1, 256),), -0.2, 0.2)), 6.103515609590104e-11, 2.441406243836042e-10)
    head_b = gaussian(arg_keys[21], (PATCH,), 0.2, 1.25, (), jnp.float32)
    headb_first = gaussian(arg_keys[22], (PATCH,), (0.02 / D), 0.00012207031, (), jnp.float32)
    headb_second = jnp.clip(jnp.exp(jax.random.uniform(arg_keys[23], (PATCH,), jnp.float32, math.log(3.8146971692576415e-10), math.log(1.5258788677030566e-09))), 3.8146971692576415e-10, 1.5258788677030566e-09)
    return dict(noisy_patches=noisy_patches, true_noise=true_noise, timesteps=timesteps, labels=labels, attn_w=attn_w, attn_mom=attn_mom, mlp_w=mlp_w, mlp_mom=mlp_mom, mod_w=mod_w, mod_mom=mod_mom, temb_w=temb_w, temb_mom=temb_mom, label_table=label_table, table_first=table_first, table_second=table_second, io_w=io_w, io_first=io_first, io_second=io_second, vec_w=vec_w, vec_first=vec_first, vec_second=vec_second, head_b=head_b, headb_first=headb_first, headb_second=headb_second)


PREC_HIGH = lax.Precision.HIGHEST
NS_A = 3.4445
NS_B = -4.775
NS_C = 2.0315
CLIP_NORM = 0.01
LR_MUON = 0.5
MOMENT_DECAY = 0.5
BETA_ONE = 0.5
BETA_TWO = 0.5
ADAM_EPS = 1e-08
LN_EPS = 1e-06

@jax.custom_vjp
def low(v):
    return lax.optimization_barrier(v.astype(jnp.bfloat16)).astype(jnp.float32)

@jax.custom_vjp
def low_back(v):
    return v

def low_keep(v):
    return (low(v), None)

def low_pass(kept, grad):
    return (grad,)

def back_keep(v):
    return (v, None)

def back_low(kept, grad):
    return (low(grad),)
low.defvjp(low_keep, low_pass)
low_back.defvjp(back_keep, back_low)

def time_features(steps_in, feat_width):
    half_width = feat_width // 2
    freq_rates = jnp.exp(-math.log(10000.0) * jnp.arange(half_width, dtype=jnp.float32) / half_width)
    phases = steps_in.astype(jnp.float32)[:, None] * freq_rates[None, :]
    return jnp.concatenate([jnp.cos(phases), jnp.sin(phases)], axis=1)

def grid_table(grid_side, feat_width):
    quarter = feat_width // 4
    freq_rates = jnp.exp(-math.log(10000.0) * jnp.arange(quarter, dtype=jnp.float32) / quarter)
    places = jnp.arange(grid_side * grid_side)
    column = (places % grid_side).astype(jnp.float32)[:, None] * freq_rates[None, :]
    row_place = (places // grid_side).astype(jnp.float32)[:, None] * freq_rates[None, :]
    return jnp.concatenate([jnp.sin(column), jnp.cos(column), jnp.sin(row_place), jnp.cos(row_place)], axis=1)

def layer_norm(values):
    center = lax.optimization_barrier(jnp.mean(values, axis=-1, keepdims=True))
    shifted = values - center
    inv_std = lax.rsqrt(lax.optimization_barrier(jnp.mean(shifted * shifted, axis=-1, keepdims=True)) + LN_EPS)
    return (shifted * inv_std, inv_std)

def keep_local(gram_list):
    return gram_list

def newton(members, reduce_fn):
    gram_list = reduce_fn(tuple((jnp.einsum('bij,bkj->bik', member, member, precision=PREC_HIGH) for member in members)))
    iterates = []
    scaled = []
    for member, gram_mat in zip(members, gram_list):
        block_norm = jnp.sqrt(jnp.einsum('bii->b', gram_mat)) + 1e-07
        iterates.append(member / block_norm[:, None, None])
        scaled.append(gram_mat / (block_norm * block_norm)[:, None, None])
    iterates = tuple(iterates)
    gram_list = tuple(scaled)
    for turn_index in range(NS_STEPS):
        if turn_index > 0:
            gram_list = reduce_fn(tuple((jnp.einsum('bij,bkj->bik', member, member, precision=PREC_HIGH) for member in iterates)))
        updated = []
        for current, gram_mat in zip(iterates, gram_list):
            once_applied = jnp.einsum('bik,bkj->bij', gram_mat, current, precision=PREC_HIGH)
            twice_applied = jnp.einsum('bik,bkj->bij', gram_mat, once_applied, precision=PREC_HIGH)
            updated.append(NS_A * current + NS_B * once_applied + NS_C * twice_applied)
        iterates = tuple(updated)
    return iterates

def adam(weight, first_old, second_old, grad_in, step_rate):
    first_new = BETA_ONE * first_old + (1.0 - BETA_ONE) * grad_in
    second_new = BETA_TWO * second_old + (1.0 - BETA_TWO) * grad_in * grad_in
    fix_one = 1.0 - BETA_ONE ** STEP
    fix_two = 1.0 - BETA_TWO ** STEP
    new_weight = weight - step_rate * (first_new / fix_one) / (jnp.sqrt(second_new / fix_two) + ADAM_EPS)
    return (new_weight, first_new, second_new)

def muon_full(weight, moment_old, grad_in):
    moment = MOMENT_DECAY * moment_old + grad_in
    slots, height, breadth = moment.shape
    blocks = moment.reshape(slots * (height // RB), RB, breadth)
    ortho = newton((blocks,), keep_local)[0].reshape(slots, height, breadth)
    return (weight - LR_MUON * ortho, moment)

def block_loss(weights, patch_vals, target, mod_now):
    attn_l, mlp_l, io_l, vec_l, head_l = weights
    fc_blocks = FF // D
    count_lat = patch_vals.shape[0]
    scale_qk = 1.0 / math.sqrt(HDIM)
    x_in = low_back(jnp.einsum('lsp,pd->lsd', patch_vals, io_l[0], precision=PREC_HIGH)) + vec_l[0] + grid_table(GRID, D)
    rows_mod = [mod_now[slot_index][:, None, :] for slot_index in range(8)]
    h_one = low(layer_norm(x_in)[0] * (1.0 + rows_mod[1]) + rows_mod[0])
    projected = jnp.einsum('lsd,kde->klse', h_one, attn_l[:3], precision=PREC_HIGH)
    q_all = low_back(low(projected[0] + vec_l[11])).reshape(count_lat, SEQ, HEADS, HDIM)
    k_all = low_back(low(projected[1])).reshape(count_lat, SEQ, HEADS, HDIM)
    v_all = low_back(low(projected[2] + vec_l[12])).reshape(count_lat, SEQ, HEADS, HDIM)
    scores = low_back(jnp.einsum('lqhd,lkhd->lhqk', q_all, k_all, precision=PREC_HIGH)) * scale_qk
    probs_low = low(jax.nn.softmax(scores, axis=-1))
    attended = jnp.einsum('lhqk,lkhd->lqhd', probs_low, v_all, precision=PREC_HIGH).reshape(count_lat, SEQ, D)
    attended = low_back(low(attended))
    attn_out = low_back(jnp.einsum('lse,de->lsd', attended, attn_l[3], precision=PREC_HIGH)) + vec_l[13]
    x_one = x_in + rows_mod[2] * attn_out
    h_two = low(layer_norm(x_one)[0] * (1.0 + rows_mod[4]) + rows_mod[3])
    pre_mlp = low_back(jnp.einsum('lsd,cde->lsce', h_two, mlp_l[:fc_blocks], precision=PREC_HIGH)) + vec_l[14:14 + fc_blocks]
    act_mlp = low(jax.nn.gelu(pre_mlp, approximate=True))
    mlp_out = low_back(jnp.einsum('lsce,cde->lsd', act_mlp, mlp_l[fc_blocks:], precision=PREC_HIGH)) + vec_l[14 + fc_blocks]
    x_two = x_one + rows_mod[5] * mlp_out
    y_low = low(layer_norm(x_two)[0] * (1.0 + rows_mod[7]) + rows_mod[6])
    predicted = low_back(jnp.einsum('lsd,pd->lsp', y_low, io_l[1], precision=PREC_HIGH)) + head_l
    pred_error = predicted - target
    return jnp.sum(pred_error * pred_error)

def reference(noisy_patches, true_noise, timesteps, labels, attn_w, attn_mom, mlp_w, mlp_mom, mod_w, mod_mom, temb_w, temb_mom, label_table, table_first, table_second, io_w, io_first, io_second, vec_w, vec_first, vec_second, head_b, headb_first, headb_second):
    group_size = 16
    groups = LATENTS // group_size
    patches = noisy_patches.astype(jnp.float32).reshape(groups, group_size, SEQ, PATCH)
    targets = true_noise.astype(jnp.float32).reshape(groups, group_size, SEQ, PATCH)

    def total_loss(attn_p, mlp_p, mod_p, temb_p, table_p, io_p, vec_p, head_p):
        attn_l, mlp_l, mod_l, temb_l = (low(attn_p), low(mlp_p), low(mod_p), low(temb_p))
        table_l, io_l, vec_l, head_l = (low(table_p), low(io_p), low(vec_p), low(head_p))
        freq_low = low(time_features(timesteps, FREQ))
        pre_time = low_back(jnp.dot(freq_low, temb_l[:, :FREQ].T, precision=PREC_HIGH)) + vec_l[1]
        hidden_time = low(jax.nn.silu(pre_time))
        cond_vec = low_back(jnp.dot(hidden_time, temb_l[:, FREQ:], precision=PREC_HIGH)) + vec_l[2] + table_l[labels]
        act_low = low(jax.nn.silu(cond_vec))
        modulation = low_back(jnp.einsum('ld,kde->kle', act_low, mod_l, precision=PREC_HIGH)) + vec_l[3:11][:, None, :]
        mods_grouped = modulation.reshape(8, groups, group_size, D).transpose(1, 0, 2, 3)
        weights = (attn_l, mlp_l, io_l, vec_l, head_l)

        def group_step(carry_sum, pieces):
            return (carry_sum + block_loss(weights, pieces[0], pieces[1], pieces[2]), None)
        loss_total, unused = lax.scan(jax.checkpoint(group_step), jnp.zeros((), jnp.float32), (patches, targets, mods_grouped))
        return loss_total / COUNT
    params = (attn_w, mlp_w, mod_w, temb_w, label_table, io_w, vec_w, head_b)
    loss, pullback = jax.vjp(total_loss, *params)
    grads = pullback(jnp.ones((), jnp.float32))
    square_sum = sum((jnp.sum(grad_in * grad_in) for grad_in in grads))
    grad_norm = jnp.sqrt(square_sum)
    factor = jnp.minimum(1.0, CLIP_NORM / (grad_norm + 1e-06))
    g_attn, g_mlp, g_mod, g_temb, g_table, g_io, g_vec, g_head = [factor * grad_in for grad_in in grads]
    attn_new, attn_moment = muon_full(attn_w, attn_mom, g_attn)
    mlp_new, mlp_moment = muon_full(mlp_w, mlp_mom, g_mlp)
    mod_new, mod_moment = muon_full(mod_w, mod_mom, g_mod)
    temb_moment = MOMENT_DECAY * temb_mom + g_temb
    left_part = temb_moment[:, :FREQ].reshape(D // RB, RB, FREQ)
    right_part = temb_moment[:, FREQ:].reshape(D // RB, RB, D)
    ortho_left, ortho_right = newton((left_part, right_part), keep_local)
    temb_new = temb_w - LR_MUON * jnp.concatenate([ortho_left.reshape(D, FREQ), ortho_right.reshape(D, D)], axis=1)
    table_new, table_first_new, table_second_new = adam(label_table, table_first, table_second, g_table, 0.3)
    io_rates = jnp.array([0.1, 0.01], jnp.float32).reshape(2, 1, 1)
    io_new, io_first_new, io_second_new = adam(io_w, io_first, io_second, g_io, io_rates)
    vec_new, vec_first_new, vec_second_new = adam(vec_w, vec_first, vec_second, g_vec, 0.05)
    headb_new, headb_first_new, headb_second_new = adam(head_b, headb_first, headb_second, g_head, 0.05)
    return (loss, grad_norm, attn_new, attn_moment, attn_new.astype(jnp.bfloat16), mlp_new, mlp_moment, mlp_new.astype(jnp.bfloat16), mod_new, mod_moment, mod_new.astype(jnp.bfloat16), temb_new, temb_moment, table_new, table_first_new, table_second_new, table_new.astype(jnp.bfloat16), io_new, io_first_new, io_second_new, vec_new, vec_first_new, vec_second_new, headb_new, headb_first_new, headb_second_new)
```

```python
import functools
import math

import jax
import jax.numpy as jnp
from jax import lax
from jax.experimental import pallas as pl
from jax.experimental.pallas import tpu as pltpu
from jax.sharding import Mesh
from jax.sharding import PartitionSpec as P

D = 1024
HDIM = 64
FREQ = 256
NCLS = 1000
PATCH = 16
GRID = 16
SEQ = 256
RB = 16
NS_STEPS = 5
STEP = 10
SHARD_SIZES = (8, 2, 4)
INTERPRET = False

HIGH = lax.Precision.HIGHEST
NS_A = 3.4445
NS_B = -4.775
NS_C = 2.0315
CLIP_NORM = 0.01
LR_MUON = 0.5
MOMENT_DECAY = 0.5
BETA_ONE = 0.5
BETA_TWO = 0.5
ADAM_EPS = 1e-08
LN_EPS = 1e-06

BF = jnp.bfloat16
F32 = jnp.float32

SHARD = ("z", "yh", "x")
PLANE = ("yh", "x", "yl")
ALL = ("z", "yh", "x", "yl", "c")


def dot(lhs, rhs, lhs_dim, rhs_dim, precision=None):
    return lax.dot_general(
        lhs,
        rhs,
        (((lhs_dim,), (rhs_dim,)), ((), ())),
        precision=precision,
        preferred_element_type=F32,
    )


def rounded(v):
    return lax.reduce_precision(v.astype(F32), 8, 7)


def exchange(v, axes):
    return lax.all_to_all(v, axes, 0, 0, tiled=True)


def swap(v, axis):
    return lax.ppermute(v, axis, [(0, 1), (1, 0)])


def in_order(index, mine, other, axis):
    return jnp.where(
        index == 0,
        jnp.concatenate([mine, other], axis=axis),
        jnp.concatenate([other, mine], axis=axis),
    )


def grid_table():
    quarter = D // 4
    rates = jnp.exp(-math.log(10000.0) * jnp.arange(quarter, dtype=F32) / quarter)
    phases = jnp.arange(GRID).astype(F32)[:, None] * rates[None, :]
    sines, cosines = jnp.sin(phases), jnp.cos(phases)
    full = (GRID, GRID, quarter)
    return jnp.concatenate(
        [
            jnp.broadcast_to(sines[None], full),
            jnp.broadcast_to(cosines[None], full),
            jnp.broadcast_to(sines[:, None], full),
            jnp.broadcast_to(cosines[:, None], full),
        ],
        axis=2,
    ).reshape(SEQ, D)


def layer_norm(values):
    center = jnp.mean(values, axis=-1, keepdims=True)
    shifted = values - center
    inv_std = lax.rsqrt(jnp.mean(shifted * shifted, axis=-1, keepdims=True) + LN_EPS)
    return (shifted * inv_std, inv_std)


def norm_back(grad_norm, normed, inv_std):
    return inv_std * (
        grad_norm
        - jnp.mean(grad_norm, axis=-1, keepdims=True)
        - normed * jnp.mean(grad_norm * normed, axis=-1, keepdims=True)
    )


def gelu_tanh(values):
    return jax.nn.gelu(values, approximate=True)


def newton_kernel(gram_ref, norm_ref, out_ref):
    size = gram_ref.shape[-1]
    rows = lax.broadcasted_iota(jnp.int32, (size, size), 0)
    cols = lax.broadcasted_iota(jnp.int32, (size, size), 1)
    eye = (rows == cols).astype(F32)
    groups = gram_ref.shape[0]
    inv = [1.0 / norm_ref[g] for g in range(groups)]
    quad = [gram_ref[g] * (inv[g] * inv[g]) for g in range(groups)]
    total = [None] * groups

    def mul(a, b):
        return jnp.dot(a, b, precision=HIGH, preferred_element_type=F32)

    for turn in range(NS_STEPS):
        poly = [NS_A * eye + NS_B * q + NS_C * mul(q, q) for q in quad]
        total = [p if turn == 0 else mul(p, t) for p, t in zip(poly, total)]
        if turn < NS_STEPS - 1:
            half = [mul(p, q) for p, q in zip(poly, quad)]
            quad = [mul(h, p) for h, p in zip(half, poly)]
    for g in range(groups):
        out_ref[g] = total[g] * inv[g]


def newton_maps(grams):
    size = 8 * RB
    groups = grams.shape[0] // 8
    norms = jnp.sqrt(jnp.einsum("bii->b", grams)) + 1e-07
    place = jnp.arange(size) // RB
    same = (place[:, None] == place[None, :])[None]
    tiled = jnp.tile(grams.reshape(groups, size, RB), (1, 1, 8))
    blocks = jnp.where(same, tiled, 0.0)
    norm_rows = jnp.broadcast_to(
        jnp.repeat(norms, RB).reshape(groups, size, 1), (groups, size, size)
    )
    return pl.pallas_call(
        newton_kernel,
        out_shape=jax.ShapeDtypeStruct((groups, size, size), F32),
        interpret=INTERPRET,
    )(blocks, norm_rows)


def adam(weight, first_old, second_old, grad_in, step_rate):
    first_new = BETA_ONE * first_old + (1.0 - BETA_ONE) * grad_in
    second_new = BETA_TWO * second_old + (1.0 - BETA_TWO) * grad_in * grad_in
    fix_one = 1.0 - BETA_ONE**STEP
    fix_two = 1.0 - BETA_TWO**STEP
    new_weight = weight - step_rate * (first_new / fix_one) / (
        jnp.sqrt(second_new / fix_two) + ADAM_EPS
    )
    return (new_weight, first_new, second_new)


def heads_of(v):
    return v.reshape(SEQ, -1, HDIM)


def raw_scores(q_low, k_low):
    return jnp.einsum(
        "qhd,khd->hqk", heads_of(q_low), heads_of(k_low), preferred_element_type=F32
    ) * (1.0 / math.sqrt(HDIM))


def attend(q_low, k_low, v_low):
    scores = raw_scores(q_low, k_low)
    peak = jnp.max(scores, axis=-1, keepdims=True)
    log_total = peak + jnp.log(jnp.sum(jnp.exp(scores - peak), axis=-1, keepdims=True))
    probs = jnp.exp(scores - log_total).astype(BF)
    out = jnp.einsum("hqk,khd->qhd", probs, heads_of(v_low), preferred_element_type=F32)
    return out.reshape(q_low.shape).astype(BF), log_total


def attend_back(q_low, k_low, v_low, log_total, d_att):
    shape = q_low.shape
    probs = jnp.exp(raw_scores(q_low, k_low) - log_total)
    d_heads = heads_of(d_att)
    d_probs = jnp.einsum("qhd,khd->hqk", d_heads, heads_of(v_low), preferred_element_type=F32)
    d_value = jnp.einsum("hqk,qhd->khd", probs.astype(BF), d_heads, preferred_element_type=F32)
    row_dot = jnp.sum(d_probs * probs, axis=-1, keepdims=True)
    d_raw = (probs * (d_probs - row_dot) * (1.0 / math.sqrt(HDIM))).astype(BF)
    d_query = jnp.einsum("hqk,khd->qhd", d_raw, heads_of(k_low), preferred_element_type=F32)
    d_key = jnp.einsum("hqk,qhd->khd", d_raw, heads_of(q_low), preferred_element_type=F32)
    return (
        d_query.reshape(shape).astype(BF),
        d_key.reshape(shape).astype(BF),
        d_value.reshape(shape).astype(BF),
    )


def on_device(
    noisy_patches,
    true_noise,
    timesteps,
    labels,
    attn_w,
    attn_mom,
    mlp_w,
    mlp_mom,
    mod_w,
    mod_mom,
    temb_w,
    temb_mom,
    label_table,
    table_first,
    table_second,
    io_w,
    io_first,
    io_second,
    vec_w,
    vec_first,
    vec_second,
    head_b,
    headb_first,
    headb_second,
):
    n_shard = lax.axis_size(SHARD)
    n_all = lax.axis_size(ALL)
    n_plane = lax.axis_size(PLANE)
    count_all = n_all * SEQ * PATCH
    yl, core = lax.axis_index("yl"), lax.axis_index("c")
    sub = 2 * yl + core
    shard = lax.axis_index(SHARD)
    half = D // 2
    quarter = D // 4
    wide = 4 * half

    attn_low = lax.dynamic_slice_in_dim(attn_w, core * quarter, quarter, axis=2).astype(BF)
    mlp_low = lax.dynamic_slice_in_dim(mlp_w, yl * 4, 4, axis=0).astype(BF)
    own_rows = jnp.concatenate(
        [
            attn_low.transpose(1, 0, 2).reshape(RB, 4 * quarter),
            mlp_low.transpose(1, 0, 2).reshape(RB, wide),
        ],
        axis=1,
    )
    plane_rows = exchange(
        jnp.broadcast_to(own_rows[None], (n_plane,) + own_rows.shape), PLANE
    ).reshape(n_plane // 2, 2, RB, -1)
    z_rows = n_plane // 2 * RB
    attn_z = (
        plane_rows[..., : 4 * quarter]
        .reshape(n_plane // 2, 2, RB, 4, quarter)
        .transpose(0, 2, 3, 1, 4)
        .reshape(z_rows, wide)
    )
    first_z = plane_rows[:, 0, :, 4 * quarter :].reshape(z_rows, wide)
    second_z = plane_rows[:, 1, :, 4 * quarter :].reshape(z_rows, wide)
    attn_mine = lax.all_gather(attn_z, "z", axis=0, tiled=True)
    first_mine = lax.all_gather(first_z, "z", axis=0, tiled=True)
    second_mine = lax.all_gather(second_z, "z", axis=0, tiled=True)
    attn_halves = (attn_mine, swap(attn_mine, "c"))
    first_halves = (first_mine, swap(first_mine, "c"))
    second_halves = (second_mine, swap(second_mine, "c"))

    label_own = lax.dynamic_index_in_dim(labels, sub, keepdims=False)
    time_own = lax.dynamic_index_in_dim(timesteps, sub, keepdims=False)
    vec_cols = vec_w.shape[1]
    lanes_io = vec_w.shape[0]
    lanes_int = lanes_io + 2 * PATCH
    lanes_mod = 64
    lanes_all = 128
    ints = jnp.stack([label_own // 32, label_own % 32, time_own // 32, time_own % 32])
    common = jnp.concatenate(
        [
            vec_w.T.astype(BF),
            io_w.reshape(2 * PATCH, vec_cols).T.astype(BF),
            jnp.broadcast_to(ints.astype(BF)[None], (vec_cols, 4)),
            jnp.zeros((vec_cols, lanes_mod - lanes_int - 4), BF),
        ],
        axis=1,
    )
    mod_own = mod_w.astype(BF)
    mod_cols = (
        lax.dynamic_slice_in_dim(mod_own, sub * 4, 4, axis=1)
        .reshape(4, 2, 4, n_shard, RB)
        .transpose(3, 0, 2, 1, 4)
        .reshape(n_all, 4, 2 * RB)
    )
    sent = jnp.concatenate(
        [
            jnp.broadcast_to(common[None], (n_all,) + common.shape),
            mod_cols,
            jnp.zeros((n_all, 4, lanes_all - lanes_mod - 2 * RB), BF),
        ],
        axis=2,
    )
    got = exchange(sent, ALL)
    marks = got[:, 0, lanes_int : lanes_int + 4].astype(F32)
    labels_all = (marks[:, 0] * 32.0 + marks[:, 1]).astype(jnp.int32)
    times_all = marks[:, 2] * 32.0 + marks[:, 3]
    by_feature = got.reshape(D, lanes_all)
    by_row = by_feature[:, :lanes_int].astype(F32).T
    vec_f = by_row[:lanes_io]
    io_low = by_row[lanes_io:lanes_int].astype(BF)
    mod_col = by_feature[:, lanes_mod : lanes_mod + 2 * RB]
    own_features = lax.dynamic_slice_in_dim(by_feature, shard * RB, RB, axis=0)[
        :, :lanes_io
    ].astype(F32)
    own_mod_bias = lax.dynamic_slice_in_dim(own_features, 3 + 2 * sub, 2, axis=1)

    rates = jnp.exp(-math.log(10000.0) * jnp.arange(FREQ // 2, dtype=F32) / (FREQ // 2))
    phases = rates[:, None] * times_all[None, :]
    freq_t = jnp.concatenate([jnp.cos(phases), jnp.sin(phases)], axis=0).astype(BF)
    temb_low = temb_w.astype(BF)
    pre_t = dot(temb_low[:, :FREQ], freq_t, 1, 0) + own_features[:, 1:2]
    hid_t = jax.nn.silu(pre_t).astype(BF)
    temb_cols = lax.dynamic_slice_in_dim(
        temb_low[:, FREQ:].reshape(RB, n_shard, 4, vec_cols), sub, 1, axis=2
    ).reshape(RB, n_shard * vec_cols)
    cond_parts = dot(temb_cols, hid_t, 0, 0)
    cond_parts = exchange(cond_parts.reshape(n_shard, vec_cols, n_all), SHARD)
    onehot = (labels_all[:, None] == jnp.arange(NCLS)[None, :]).astype(BF)
    label_rows = dot(label_table.astype(BF), onehot, 0, 1)
    cond_t = jnp.sum(cond_parts, axis=0) + label_rows + rounded(vec_w[2])[:, None]
    act_own = jax.nn.silu(cond_t).astype(BF)
    act_t = exchange(jnp.broadcast_to(act_own[None], (n_all,) + act_own.shape), ALL).reshape(
        D, n_all
    )
    mods_sent = dot(act_t, mod_col, 0, 0) + own_mod_bias.T.reshape(1, 2 * RB)
    mods = (
        exchange(mods_sent, ALL)
        .reshape(n_shard, 8, RB)
        .transpose(1, 0, 2)
        .reshape(8, 1, D)
    )

    patch_vals = lax.dynamic_index_in_dim(noisy_patches, sub, keepdims=False).reshape(SEQ, PATCH)
    target = lax.dynamic_index_in_dim(true_noise, sub, keepdims=False).reshape(SEQ, PATCH)
    head_low = rounded(head_b)
    x_in = dot(patch_vals, io_low[:PATCH], 1, 0) + vec_f[0] + grid_table()
    norm_one, inv_one = layer_norm(x_in)
    h_one = (norm_one * (1.0 + mods[1]) + mods[0]).astype(BF)
    own_half = (core, 1 - core)

    def attn_bias(row, which):
        rows = vec_f[row].reshape(2, 2, quarter)
        return lax.dynamic_index_in_dim(rows, which, axis=1, keepdims=False).reshape(half)

    qkv = []
    attended = []
    log_totals = []
    attn_out = vec_f[13]
    for weight, which in zip(attn_halves, own_half):
        proj = dot(h_one, weight[:, : 3 * half], 1, 0)
        q_low = (proj[:, :half] + attn_bias(11, which)).astype(BF)
        k_low = proj[:, half : 2 * half].astype(BF)
        v_low = (proj[:, 2 * half :] + attn_bias(12, which)).astype(BF)
        att, log_total = attend(q_low, k_low, v_low)
        qkv.append((q_low, k_low, v_low))
        attended.append(att)
        log_totals.append(log_total)
        attn_out = attn_out + dot(att, weight[:, 3 * half :], 1, 1)
    x_one = x_in + mods[2] * attn_out
    norm_two, inv_two = layer_norm(x_one)
    h_two = (norm_two * (1.0 + mods[4]) + mods[3]).astype(BF)
    pre_mlp = []
    act_mlp = []
    mlp_out = vec_f[18]
    for first, second, which in zip(first_halves, second_halves, own_half):
        bias = lax.dynamic_slice_in_dim(vec_f[14:18], which * half, half, axis=1).reshape(wide)
        pre = dot(h_two, first, 1, 0) + bias
        act = gelu_tanh(pre).astype(BF)
        pre_mlp.append(pre)
        act_mlp.append(act)
        mlp_out = mlp_out + dot(act, second, 1, 1)
    x_two = x_one + mods[5] * mlp_out
    norm_fin, inv_fin = layer_norm(x_two)
    y_low = (norm_fin * (1.0 + mods[7]) + mods[6]).astype(BF)
    pred_error = dot(y_low, io_low[PATCH:], 1, 1) + head_low - target.astype(F32)
    loss_own = jnp.sum(pred_error * pred_error)

    d_pred = pred_error * (2.0 / count_all)
    d_pred_low = d_pred.astype(BF)
    grad_head = dot(d_pred_low, y_low, 0, 0)
    grad_hb = jnp.sum(d_pred, axis=0)
    d_y = dot(d_pred_low, io_low[PATCH:], 1, 0)
    d_shift_fin = jnp.sum(d_y, axis=0)
    d_scale_fin = jnp.sum(d_y * norm_fin, axis=0)
    d_two = norm_back(d_y * (1.0 + mods[7]), norm_fin, inv_fin)
    d_gate_two = jnp.sum(d_two * mlp_out, axis=0)
    d_mlp = mods[5] * d_two
    d_mlp_low = d_mlp.astype(BF)
    grad_bfc = jnp.sum(d_mlp, axis=0)
    grad_second = [dot(d_mlp_low, act, 0, 0).astype(BF) for act in act_mlp]
    second_sum = chip_sum(grad_second)
    second_z = lax.psum_scatter(second_sum, "z", scatter_dimension=0, tiled=True)
    d_pre_low = []
    hid_bias = []
    d_h_two = 0.0
    for pre, first, second in zip(pre_mlp, first_halves, second_halves):
        d_act = dot(d_mlp_low, second, 1, 0)
        d_pre = jax.vjp(gelu_tanh, pre)[1](d_act)[0]
        hid_bias.append(jnp.sum(d_pre, axis=0).reshape(4, half))
        d_pre_low.append(d_pre.astype(BF))
        d_h_two = d_h_two + dot(d_pre_low[-1], first, 1, 1)
    grad_first = [dot(h_two, d, 0, 0).astype(BF) for d in d_pre_low]
    first_sum = chip_sum(grad_first)
    first_z = lax.psum_scatter(first_sum, "z", scatter_dimension=0, tiled=True)
    grad_bhid = in_order(core, hid_bias[0], hid_bias[1], 1)
    d_shift_two = jnp.sum(d_h_two, axis=0)
    d_scale_two = jnp.sum(d_h_two * norm_two, axis=0)
    d_one = d_two + norm_back(d_h_two * (1.0 + mods[4]), norm_two, inv_two)
    d_gate_one = jnp.sum(d_one * attn_out, axis=0)
    d_attn = mods[2] * d_one
    d_attn_low = d_attn.astype(BF)
    grad_bout = jnp.sum(d_attn, axis=0)
    grad_attn = []
    qv_bias = []
    d_h_one = 0.0
    for weight, (q_low, k_low, v_low), att, log_total in zip(
        attn_halves, qkv, attended, log_totals
    ):
        d_att = dot(d_attn_low, weight[:, 3 * half :], 1, 0).astype(BF)
        d_query, d_key, d_value = attend_back(q_low, k_low, v_low, log_total, d_att)
        d_proj = jnp.concatenate([d_query, d_key, d_value], axis=1)
        grad_attn.append(
            jnp.concatenate(
                [
                    dot(h_one, d_proj, 0, 0).astype(BF),
                    dot(d_attn_low, att, 0, 0).astype(BF),
                ],
                axis=1,
            )
        )
        qv_bias.append(
            jnp.stack(
                [
                    jnp.sum(d_query.astype(F32), axis=0),
                    jnp.sum(d_value.astype(F32), axis=0),
                ]
            ).reshape(2, 2, 1, quarter)
        )
        d_h_one = d_h_one + dot(d_proj, weight[:, : 3 * half], 1, 1)
    attn_sum = chip_sum(grad_attn)
    attn_zg = lax.psum_scatter(attn_sum, "z", scatter_dimension=0, tiled=True)
    grad_bqv = in_order(core, qv_bias[0], qv_bias[1], 2).reshape(2, D)
    d_shift_one = jnp.sum(d_h_one, axis=0)
    d_scale_one = jnp.sum(d_h_one * norm_one, axis=0)
    d_in = d_one + norm_back(d_h_one * (1.0 + mods[1]), norm_one, inv_one)
    grad_patch = dot(patch_vals, d_in.astype(BF), 0, 0)
    grad_bpatch = jnp.sum(d_in, axis=0)
    d_mods = jnp.stack(
        [
            d_shift_one,
            d_scale_one,
            d_gate_one,
            d_shift_two,
            d_scale_two,
            d_gate_two,
            d_shift_fin,
            d_scale_fin,
        ]
    )

    dmod_sent = jnp.broadcast_to(
        d_mods.astype(BF).reshape(1, 4, 2 * D), (n_shard, 4, 2 * D)
    ).reshape(n_all, 2 * D)
    dmod_all = exchange(dmod_sent, ALL)
    mod_sub = lax.dynamic_slice_in_dim(mod_own, 2 * sub, 2, axis=0)
    act_rows = lax.dynamic_slice_in_dim(act_t, shard * RB, RB, axis=0)
    grad_mod = dot(act_rows, dmod_all, 1, 0).reshape(RB, 2, D).transpose(1, 0, 2)
    d_act = dot(mod_sub.transpose(1, 0, 2).reshape(RB, 2 * D), dmod_all, 1, 1)
    d_act = lax.psum(d_act, ("yl", "c"))
    d_act = lax.dynamic_slice_in_dim(d_act, sub * vec_cols, vec_cols, axis=0)
    d_cond = jax.vjp(jax.nn.silu, cond_t)[1](d_act)[0]
    grad_table = dot(onehot.astype(F32), d_cond, 0, 1, HIGH)
    grad_bt_two = jnp.sum(d_cond, axis=1)
    d_cond_low = d_cond.astype(BF)
    d_cond_t = exchange(
        jnp.broadcast_to(d_cond_low[None], (n_all,) + d_cond_low.shape), ALL
    ).reshape(D, n_all)
    d_hidden = dot(temb_low[:, FREQ:], d_cond_t, 1, 0)
    d_pre_time = jax.vjp(jax.nn.silu, pre_t)[1](d_hidden)[0]
    grad_bt_one = lax.dynamic_slice_in_dim(
        jnp.sum(d_pre_time, axis=1), sub * vec_cols, vec_cols, axis=0
    )
    grad_temb = jnp.concatenate(
        [dot(d_pre_time.astype(BF), freq_t, 1, 1), dot(hid_t, d_cond_t, 1, 1)], axis=1
    )

    small = jnp.concatenate(
        [
            grad_bpatch[None],
            d_mods,
            grad_bqv,
            grad_bout[None],
            grad_bhid,
            grad_bfc[None],
            grad_patch,
            grad_head,
        ],
        axis=0,
    )
    n_small = small.shape[0]
    small_sent = (
        jnp.pad(small, ((0, 64 - n_small), (0, 0))).T.reshape(n_all, vec_cols, 64)
    )
    small_own = jnp.sum(exchange(small_sent, ALL), axis=0).T
    vec_s = jnp.concatenate(
        [small_own[:1], grad_bt_one[None], grad_bt_two[None], small_own[1:17]], axis=0
    )
    io_s = small_own[17:n_small].reshape(2, PATCH, vec_cols)

    grads_sent = jnp.concatenate(
        [
            attn_zg.reshape(n_plane // 2, RB, 4, 2, quarter)
            .transpose(0, 3, 1, 2, 4)
            .reshape(n_plane // 2, 2, RB, 4 * quarter),
            jnp.stack(
                [
                    first_z.reshape(n_plane // 2, RB, wide),
                    second_z.reshape(n_plane // 2, RB, wide),
                ],
                axis=1,
            ),
        ],
        axis=3,
    ).reshape(n_plane, RB, 4 * quarter + wide)
    grads_own = jnp.sum(exchange(grads_sent, PLANE).astype(F32), axis=0)
    attn_q = grads_own[:, : 4 * quarter].reshape(RB, 4, quarter).transpose(1, 0, 2)
    mlp_q = grads_own[:, 4 * quarter :].reshape(RB, 4, half).transpose(1, 0, 2)
    attn_s = in_order(core, attn_q, swap(attn_q, "c"), 2)
    mlp_s = in_order(yl, mlp_q, swap(mlp_q, "yl"), 0)
    mod_s = lax.all_gather(
        lax.all_gather(grad_mod, "c", axis=0, tiled=True), "yl", axis=0, tiled=True
    )

    local_square = (
        jnp.sum(grads_own * grads_own)
        + jnp.sum(grad_mod * grad_mod)
        + 0.25 * jnp.sum(grad_temb * grad_temb)
        + jnp.sum(grad_table * grad_table)
        + jnp.sum(io_s * io_s)
        + jnp.sum(vec_s * vec_s)
    )
    sums = jnp.concatenate([local_square[None], loss_own[None], grad_hb])
    sums = jnp.pad(sums, (0, 128 - sums.shape[0]))
    sums = jnp.sum(exchange(jnp.broadcast_to(sums[None], (n_all, 128)), ALL), axis=0)
    loss = sums[1] / count_all
    head_all = sums[2 : 2 + PATCH]
    grad_norm = jnp.sqrt(sums[0] + jnp.sum(head_all * head_all))
    factor = jnp.minimum(1.0, CLIP_NORM / (grad_norm + 1e-06))

    attn_moment = MOMENT_DECAY * attn_mom + factor * attn_s
    mlp_moment = MOMENT_DECAY * mlp_mom + factor * mlp_s
    mod_moment = MOMENT_DECAY * mod_mom + factor * mod_s
    temb_moment = MOMENT_DECAY * temb_mom + factor * grad_temb
    gram_attn = jnp.einsum("bij,bkj->bik", attn_moment, attn_moment, precision=HIGH)
    gram_mlp = jnp.einsum("bij,bkj->bik", mlp_moment, mlp_moment, precision=HIGH)
    gram_mod = jnp.einsum("bij,bkj->bik", mod_moment, mod_moment, precision=HIGH)
    temb_left, temb_right = temb_moment[:, :FREQ], temb_moment[:, FREQ:]
    gram_left = dot(temb_left, temb_left, 1, 1, HIGH)[None]
    gram_right = dot(temb_right, temb_right, 1, 1, HIGH)[None]
    gram_attn = gram_attn + swap(gram_attn, "yl")
    gram_mlp = gram_mlp + swap(gram_mlp, "c")
    maps = newton_maps(
        jnp.concatenate(
            [gram_attn, gram_left, gram_right, jnp.zeros((2, RB, RB), F32), gram_mlp, gram_mod]
        )
    )
    n_attn = 4 * RB
    attn_ortho = dot(
        maps[0, :n_attn, :n_attn], attn_moment.reshape(n_attn, half), 1, 0, HIGH
    ).reshape(attn_moment.shape)
    left_ortho = dot(
        maps[0, n_attn : n_attn + RB, n_attn : n_attn + RB], temb_left, 1, 0, HIGH
    )
    right_ortho = dot(
        maps[0, n_attn + RB : n_attn + 2 * RB, n_attn + RB : n_attn + 2 * RB],
        temb_right,
        1,
        0,
        HIGH,
    )
    mlp_ortho = dot(maps[1], mlp_moment.reshape(8 * RB, half), 1, 0, HIGH).reshape(
        mlp_moment.shape
    )
    mod_ortho = dot(maps[2], mod_moment.reshape(8 * RB, D), 1, 0, HIGH).reshape(mod_moment.shape)
    attn_new = attn_w - LR_MUON * attn_ortho
    mlp_new = mlp_w - LR_MUON * mlp_ortho
    mod_new = mod_w - LR_MUON * mod_ortho
    temb_new = temb_w - LR_MUON * jnp.concatenate([left_ortho, right_ortho], axis=1)
    table_new, table_first_new, table_second_new = adam(
        label_table, table_first, table_second, factor * grad_table, 0.3
    )
    io_rates = jnp.array([0.1, 0.01], F32).reshape(2, 1, 1)
    io_new, io_first_new, io_second_new = adam(io_w, io_first, io_second, factor * io_s, io_rates)
    vec_new, vec_first_new, vec_second_new = adam(
        vec_w, vec_first, vec_second, factor * vec_s, 0.05
    )
    headb_new, headb_first_new, headb_second_new = adam(
        head_b, headb_first, headb_second, factor * head_all, 0.05
    )
    return (
        loss,
        grad_norm,
        attn_new,
        attn_moment,
        attn_new.astype(BF),
        mlp_new,
        mlp_moment,
        mlp_new.astype(BF),
        mod_new,
        mod_moment,
        mod_new.astype(BF),
        temb_new,
        temb_moment,
        table_new,
        table_first_new,
        table_second_new,
        table_new.astype(BF),
        io_new,
        io_first_new,
        io_second_new,
        vec_new,
        vec_first_new,
        vec_second_new,
        headb_new,
        headb_first_new,
        headb_second_new,
    )


def chip_sum(halves):
    mine, other = halves
    return (mine.astype(F32) + swap(other, "c").astype(F32)).astype(BF)


def solution(mesh):
    fine = Mesh(mesh.devices.reshape(SHARD_SIZES + (2, 2)), ALL)
    lat = P(SHARD, None)
    one = P(SHARD)
    attn = P(None, SHARD, "yl")
    mlp = P(None, SHARD, "c")
    mod = P(None, SHARD, None)
    temb = P(SHARD, None)
    flat = P(None, ALL)
    io = P(None, None, ALL)
    rep = P()
    return jax.shard_map(
        on_device,
        mesh=fine,
        in_specs=(lat, lat, one, one, attn, attn, mlp, mlp, mod, mod, temb, temb)
        + (flat,) * 3
        + (io,) * 3
        + (flat,) * 3
        + (rep,) * 3,
        out_specs=(rep, rep)
        + (attn,) * 3
        + (mlp,) * 3
        + (mod,) * 3
        + (temb,) * 2
        + (flat,) * 4
        + (io,) * 3
        + (flat,) * 3
        + (rep,) * 3,
        check_vma=False,
    )
```

```python
import functools
import math

import jax
import jax.numpy as jnp
from jax import lax
from jax.experimental import pallas as pl
from jax.experimental.pallas import tpu as pltpu
from jax.sharding import Mesh
from jax.sharding import PartitionSpec as P

D = 1024
HDIM = 64
FREQ = 256
NCLS = 1000
PATCH = 16
GRID = 16
SEQ = 256
RB = 16
NS_STEPS = 5
STEP = 10
SHARD_SIZES = (8, 2, 4)
INTERPRET = False

HIGH = lax.Precision.HIGHEST
NS_A = 3.4445
NS_B = -4.775
NS_C = 2.0315
CLIP_NORM = 0.01
LR_MUON = 0.5
MOMENT_DECAY = 0.5
BETA_ONE = 0.5
BETA_TWO = 0.5
ADAM_EPS = 1e-08
LN_EPS = 1e-06

BF = jnp.bfloat16
F32 = jnp.float32

SHARD = ("z", "yh", "x")
PLANE = ("yh", "x", "yl")
ALL = ("z", "yh", "x", "yl", "c")


def dot(lhs, rhs, lhs_dim, rhs_dim, precision=None):
    return lax.dot_general(
        lhs,
        rhs,
        (((lhs_dim,), (rhs_dim,)), ((), ())),
        precision=precision,
        preferred_element_type=F32,
    )


def rounded(v):
    return lax.reduce_precision(v.astype(F32), 8, 7)


def exchange(v, axes):
    return lax.all_to_all(v, axes, 0, 0)


def to_all(v, axes):
    return exchange(jnp.broadcast_to(v[None], (lax.axis_size(axes),) + v.shape), axes)


def after(v, *others):
    return lax.optimization_barrier((v,) + others)[0]


def swap(v, axis):
    return lax.ppermute(v, axis, [(0, 1), (1, 0)])


def shift(v, axes, by):
    size = lax.axis_size(axes)
    return lax.ppermute(v, axes, [(i, (i + by) % size) for i in range(size)])


def gather_first(v, axes):
    if lax.axis_size(axes) == 2:
        return (shift(v, axes, 1),)
    return shift(v, axes, 1), shift(v, axes, -1)


def gather_rest(v, axes, got):
    if lax.axis_size(axes) == 2:
        return (v,) + got
    before, next_ = got
    cut = v.shape[0] // 2
    across = jnp.concatenate([shift(before[:cut], axes, 1), shift(next_[cut:], axes, -1)], axis=0)
    return v, next_, across, before


def all_after(values, *others):
    return lax.optimization_barrier(tuple(values) + others)[: len(values)]


def reduce_first(piece, axes):
    if lax.axis_size(axes) == 2:
        return ()
    across = piece(2)
    cut = across.shape[0] // 2
    return shift(across[:cut], axes, 1), shift(across[cut:], axes, -1)


def reduce_rest(piece, axes, got):
    if lax.axis_size(axes) == 2:
        return piece(0).astype(F32) + shift(piece(1), axes, 1).astype(F32)
    from_before, from_after = got
    cut = from_before.shape[0]
    up, down = piece(1), piece(3)
    up = jnp.concatenate([added(up[:cut], from_before), up[cut:]], axis=0)
    down = jnp.concatenate([down[:cut], added(down[cut:], from_after)], axis=0)
    from_before = shift(up, axes, 1).astype(F32)
    from_after = shift(down, axes, -1).astype(F32)
    return piece(0).astype(F32) + from_before + from_after


def added(one, two):
    return (one.astype(F32) + two.astype(F32)).astype(BF)


def placed(blocks, index, size, axis):
    shape = list(blocks[0].shape)
    shape[axis] *= size
    out = jnp.zeros(shape, blocks[0].dtype)
    for r, block in enumerate(blocks):
        where = lax.rem(index + r, size) * blocks[0].shape[axis]
        out = lax.dynamic_update_slice_in_dim(out, block, where, axis)
    return out


def in_order(index, mine, other, axis):
    return jnp.where(
        index == 0,
        jnp.concatenate([mine, other], axis=axis),
        jnp.concatenate([other, mine], axis=axis),
    )


def place_y(blocks, y_at):
    first, _, rows, cols = blocks[0].shape
    out = jnp.zeros((first, 2, rows, 2 * cols), blocks[0].dtype)
    for r, block in enumerate(blocks):
        where = lax.rem(y_at + r, 4)
        out = lax.dynamic_update_slice(out, block, (0, where // 2, 0, where % 2 * cols))
    return out


def join_y(low, high):
    cut = 3 * low.shape[-1] // 4
    return jnp.concatenate(
        [low[..., :cut], high[..., :cut], low[..., cut:], high[..., cut:]], axis=-1
    )


def split_y(v, side):
    width = v.shape[-1] // 8
    return jnp.concatenate(
        [
            v[..., 3 * side * width : 3 * (side + 1) * width],
            v[..., (6 + side) * width : (7 + side) * width],
        ],
        axis=-1,
    )


def gather_direct(v, axes):
    return [v] + [shift(v, axes, -by) for by in range(1, lax.axis_size(axes))]


def in_ring_order(blocks, index):
    size = len(blocks)
    return lax.dynamic_slice_in_dim(
        jnp.concatenate(blocks + blocks, axis=0), lax.rem(size - index, size), size, axis=0
    )


def grid_table():
    quarter = D // 4
    rates = jnp.exp(-math.log(10000.0) * jnp.arange(quarter, dtype=F32) / quarter)
    phases = jnp.arange(GRID).astype(F32)[:, None] * rates[None, :]
    sines, cosines = jnp.sin(phases), jnp.cos(phases)
    full = (GRID, GRID, quarter)
    return jnp.concatenate(
        [
            jnp.broadcast_to(sines[None], full),
            jnp.broadcast_to(cosines[None], full),
            jnp.broadcast_to(sines[:, None], full),
            jnp.broadcast_to(cosines[:, None], full),
        ],
        axis=2,
    ).reshape(SEQ, D)


def layer_norm(values):
    center = jnp.mean(values, axis=-1, keepdims=True)
    shifted = values - center
    inv_std = lax.rsqrt(jnp.mean(shifted * shifted, axis=-1, keepdims=True) + LN_EPS)
    return (shifted * inv_std, inv_std)


def norm_back(grad_norm, normed, inv_std):
    return inv_std * (
        grad_norm
        - jnp.mean(grad_norm, axis=-1, keepdims=True)
        - normed * jnp.mean(grad_norm * normed, axis=-1, keepdims=True)
    )


def gelu_tanh(values):
    return jax.nn.gelu(values, approximate=True)


def newton_kernel(gram_ref, norm_ref, out_ref):
    size = gram_ref.shape[-1]
    rows = lax.broadcasted_iota(jnp.int32, (size, size), 0)
    cols = lax.broadcasted_iota(jnp.int32, (size, size), 1)
    eye = (rows == cols).astype(F32)
    groups = gram_ref.shape[0]
    inv = [1.0 / norm_ref[g] for g in range(groups)]
    quad = [gram_ref[g] * (inv[g] * inv[g]) for g in range(groups)]
    total = [None] * groups

    def mul(a, b):
        return jnp.dot(a, b, precision=HIGH, preferred_element_type=F32)

    for turn in range(NS_STEPS):
        poly = [NS_A * eye + NS_B * q + NS_C * mul(q, q) for q in quad]
        total = [p if turn == 0 else mul(p, t) for p, t in zip(poly, total)]
        if turn < NS_STEPS - 1:
            half = [mul(p, q) for p, q in zip(poly, quad)]
            quad = [mul(h, p) for h, p in zip(half, poly)]
    for g in range(groups):
        out_ref[g] = total[g] * inv[g]


def newton_maps(grams):
    size = 8 * RB
    groups = grams.shape[0] // 8
    norms = jnp.sqrt(jnp.einsum("bii->b", grams)) + 1e-07
    place = jnp.arange(size) // RB
    same = (place[:, None] == place[None, :])[None]
    tiled = jnp.tile(grams.reshape(groups, size, RB), (1, 1, 8))
    blocks = jnp.where(same, tiled, 0.0)
    norm_rows = jnp.broadcast_to(
        jnp.repeat(norms, RB).reshape(groups, size, 1), (groups, size, size)
    )
    return pl.pallas_call(
        newton_kernel,
        out_shape=jax.ShapeDtypeStruct((groups, size, size), F32),
        interpret=INTERPRET,
    )(blocks, norm_rows)


def adam(weight, first_old, second_old, grad_in, step_rate):
    first_new = BETA_ONE * first_old + (1.0 - BETA_ONE) * grad_in
    second_new = BETA_TWO * second_old + (1.0 - BETA_TWO) * grad_in * grad_in
    fix_one = 1.0 - BETA_ONE**STEP
    fix_two = 1.0 - BETA_TWO**STEP
    new_weight = weight - step_rate * (first_new / fix_one) / (
        jnp.sqrt(second_new / fix_two) + ADAM_EPS
    )
    return (new_weight, first_new, second_new)


def across_rows(lhs, rhs):
    return dot(lhs, rhs, 1, 1)


def head_probs(q, k, side):
    lane = lax.broadcasted_iota(jnp.int32, (1, 2 * HDIM), 1)
    mask = (lane // HDIM == side).astype(F32)
    scores = across_rows((q.astype(F32) * mask).astype(BF), k) * (1.0 / math.sqrt(HDIM))
    grown = jnp.exp(scores - jnp.max(scores, axis=-1, keepdims=True))
    return grown / jnp.sum(grown, axis=-1, keepdims=True), mask


def attend_kernel(*refs):
    for half in range(2):
        q, k, v = (r[...] for r in refs[3 * half : 3 * half + 3])
        out = 0.0
        for side in range(2):
            probs, mask = head_probs(q, k, side)
            out = out + mask * dot(probs.astype(BF), v, 1, 0)
        refs[6 + half][...] = out.astype(BF)


def attend_back_kernel(*refs):
    block = pl.program_id(0)
    per = pl.num_programs(0) // 2
    for half in range(2):
        q, k, v, d_att = (r[...] for r in refs[4 * half : 4 * half + 4])
        d_q, d_k, d_v = 0.0, 0.0, 0.0
        for side in range(2):
            probs, mask = head_probs(q, k, side)
            d_probs = across_rows((d_att.astype(F32) * mask).astype(BF), v)
            d_v = d_v + mask * dot(probs.astype(BF), d_att, 0, 0)
            row_dot = jnp.sum(d_probs * probs, axis=-1, keepdims=True)
            d_raw = (probs * (d_probs - row_dot) * (1.0 / math.sqrt(HDIM))).astype(BF)
            d_q = d_q + mask * dot(d_raw, k, 1, 0)
            d_k = d_k + mask * dot(d_raw, q, 0, 0)
        for at, value in enumerate((d_q, d_k, d_v)):
            where = pl.multiple_of(qkv_block(block, at, per) * 2 * HDIM, 2 * HDIM)
            refs[8 + half][:, pl.ds(where, 2 * HDIM)] = value.astype(BF)


def qkv_block(j, at, per):
    return (j // per) * 3 * per + at * per + j % per


def columns(at=None, per=1):
    if at is None:
        return pl.BlockSpec((SEQ, 2 * HDIM), lambda j: (0, j))
    return pl.BlockSpec((SEQ, 2 * HDIM), lambda j: (0, qkv_block(j, at, per)))


def attend(qkv):
    width = qkv[0].shape[1] // 3
    groups = width // (2 * HDIM)
    return pl.pallas_call(
        attend_kernel,
        grid=(groups,),
        in_specs=[columns(at, groups // 2) for at in range(3)] * 2,
        out_specs=[columns()] * 2,
        out_shape=[jax.ShapeDtypeStruct((SEQ, width), BF)] * 2,
        cost_estimate=pl.CostEstimate(
            flops=16 * SEQ * SEQ * width, bytes_accessed=16 * SEQ * width, transcendentals=8 * SEQ * SEQ
        ),
        interpret=INTERPRET,
    )(*(qkv[0],) * 3, *(qkv[1],) * 3)


def attend_back(qkv, d_att):
    width = qkv[0].shape[1] // 3
    groups = width // (2 * HDIM)
    whole = pl.BlockSpec((SEQ, 3 * width), lambda j: (0, 0))
    return pl.pallas_call(
        attend_back_kernel,
        grid=(groups,),
        in_specs=([columns(at, groups // 2) for at in range(3)] + [columns()]) * 2,
        out_specs=[whole] * 2,
        out_shape=[jax.ShapeDtypeStruct((SEQ, 3 * width), BF)] * 2,
        cost_estimate=pl.CostEstimate(
            flops=40 * SEQ * SEQ * width, bytes_accessed=28 * SEQ * width, transcendentals=8 * SEQ * SEQ
        ),
        interpret=INTERPRET,
    )(*(qkv[0],) * 3, d_att[0], *(qkv[1],) * 3, d_att[1])


def on_device(
    noisy_patches,
    true_noise,
    timesteps,
    labels,
    attn_w,
    attn_mom,
    mlp_w,
    mlp_mom,
    mod_w,
    mod_mom,
    temb_w,
    temb_mom,
    label_table,
    table_first,
    table_second,
    io_w,
    io_first,
    io_second,
    vec_w,
    vec_first,
    vec_second,
    head_b,
    headb_first,
    headb_second,
):
    n_shard = lax.axis_size(SHARD)
    n_all = lax.axis_size(ALL)
    count_all = n_all * SEQ * PATCH
    yl, core = lax.axis_index("yl"), lax.axis_index("c")
    sub = 2 * yl + core
    shard = lax.axis_index(SHARD)
    half = D // 2
    quarter = D // 4
    wide = 4 * half

    n_z, n_x = lax.axis_size("z"), lax.axis_size("x")
    x_at = lax.axis_index("x")
    yh = lax.axis_index("yh")
    y_at = 2 * yh + yl
    attn_low = lax.dynamic_slice_in_dim(attn_w, core * quarter, quarter, axis=2).astype(BF)
    attn_own = attn_low.transpose(1, 0, 2).reshape(RB, 4 * quarter)
    mlp_low = (
        lax.dynamic_slice_in_dim(mlp_w.reshape(2, 4, RB, half), 2 * yl, 2, axis=1)
        .astype(BF)
        .transpose(0, 2, 1, 3)
        .reshape(2, RB, D)
    )
    z_at = lax.axis_index("z")
    second_x = in_ring_order(gather_direct(mlp_low[1][None], "x"), x_at)
    second_parts = gather_direct(second_x.reshape(1, 1, n_x * RB, D), ("yh", "yl"))
    second_y = place_y(second_parts, y_at).reshape(2 * n_x * RB, wide)
    second_mine = lax.all_gather(second_y, "z", axis=0, tiled=True)
    both_z = in_ring_order(
        gather_direct(jnp.concatenate([attn_own, mlp_low[0]], axis=1)[None], "z"), z_at
    )

    label_own = lax.dynamic_index_in_dim(labels, sub, keepdims=False)
    time_own = lax.dynamic_index_in_dim(timesteps, sub, keepdims=False)
    vec_cols = vec_w.shape[1]
    lanes_io = vec_w.shape[0]
    lanes_int = lanes_io + 2 * PATCH
    lanes_mod = 64
    lanes_all = 128
    ints = jnp.stack([label_own // 32, label_own % 32, time_own // 32, time_own % 32])
    common = jnp.concatenate(
        [
            vec_w.T.astype(BF),
            io_w.reshape(2 * PATCH, vec_cols).T.astype(BF),
            jnp.broadcast_to(ints.astype(BF)[None], (vec_cols, 4)),
            jnp.zeros((vec_cols, lanes_mod - lanes_int - 4), BF),
        ],
        axis=1,
    )
    mod_own = mod_w.astype(BF)
    mod_cols = (
        lax.dynamic_slice_in_dim(mod_own, sub * 4, 4, axis=1)
        .reshape(4, 2, 4, n_shard, RB)
        .transpose(3, 0, 2, 1, 4)
        .reshape(n_all, 4, 2 * RB)
    )
    sent = jnp.concatenate(
        [
            jnp.broadcast_to(common[None], (n_all,) + common.shape),
            mod_cols,
            jnp.zeros((n_all, 4, lanes_all - lanes_mod - 2 * RB), BF),
        ],
        axis=2,
    )
    got = exchange(sent, ALL)
    attn_own, first_own = both_z[..., :D], both_z[:, None, :, D:]
    attn_got = gather_first(attn_own, ("yh", "yl"))
    first_got = gather_first(first_own, "x")
    low_y = yl == 0
    own, next_, across, before = gather_rest(attn_own, ("yh", "yl"), attn_got)
    pair_own = join_y(jnp.where(low_y, own, before), jnp.where(low_y, next_, own))
    pair_far = join_y(jnp.where(low_y, across, next_), jnp.where(low_y, before, across))
    attn_y = in_order(yh, pair_own[:, None], pair_far[:, None], 1).reshape(2 * n_z, 1, RB, wide)
    first_x = placed(gather_rest(first_own, "x", first_got), x_at, n_x, 1).reshape(
        n_z, 1, n_x * RB, D
    )
    attn_y, first_x = all_after((attn_y, first_x), got)
    attn_got = gather_first(attn_y, "x")
    first_got = gather_first(first_x, ("yh", "yl"))
    marks = got[:, 0, lanes_int : lanes_int + 4].astype(F32)
    labels_all = (marks[:, 0] * 32.0 + marks[:, 1]).astype(jnp.int32)
    times_all = marks[:, 2] * 32.0 + marks[:, 3]
    by_feature = got.reshape(D, lanes_all)
    by_row = by_feature[:, :lanes_int].astype(F32).T
    vec_f = by_row[:lanes_io]
    io_low = by_row[lanes_io:lanes_int].astype(BF)
    mod_col = by_feature[:, lanes_mod : lanes_mod + 2 * RB]
    own_features = lax.dynamic_slice_in_dim(by_feature, shard * RB, RB, axis=0)[
        :, :lanes_io
    ].astype(F32)
    own_mod_bias = lax.dynamic_slice_in_dim(own_features, 3 + 2 * sub, 2, axis=1)

    rates = jnp.exp(-math.log(10000.0) * jnp.arange(FREQ // 2, dtype=F32) / (FREQ // 2))
    phases = rates[:, None] * times_all[None, :]
    freq_t = jnp.concatenate([jnp.cos(phases), jnp.sin(phases)], axis=0).astype(BF)
    temb_low = temb_w.astype(BF)
    pre_t = dot(temb_low[:, :FREQ], freq_t, 1, 0) + own_features[:, 1:2]
    hid_t = jax.nn.silu(pre_t).astype(BF)
    temb_cols = lax.dynamic_slice_in_dim(
        temb_low[:, FREQ:].reshape(RB, n_shard, 4, vec_cols), sub, 1, axis=2
    ).reshape(RB, n_shard * vec_cols)
    cond_parts = dot(temb_cols, hid_t, 0, 0)
    cond_parts = exchange(
        after(cond_parts.reshape(n_shard, vec_cols, n_all), second_x), SHARD
    )
    onehot = (labels_all[:, None] == jnp.arange(NCLS)[None, :]).astype(BF)
    label_rows = dot(label_table.astype(BF), onehot, 0, 1)
    cond_t = jnp.sum(cond_parts, axis=0) + label_rows + rounded(vec_w[2])[:, None]
    act_own = jax.nn.silu(cond_t).astype(BF)
    act_t = to_all(after(act_own, second_y), ALL)
    attn_mine = placed(gather_rest(attn_y, "x", attn_got), x_at, n_x, 1).reshape(D, wide)
    first_mine = place_y(gather_rest(first_x, ("yh", "yl"), first_got), y_at).reshape(D, wide)
    patch_vals = lax.dynamic_index_in_dim(noisy_patches, sub, keepdims=False).reshape(SEQ, PATCH)
    x_in = dot(patch_vals, io_low[:PATCH], 1, 0) + vec_f[0] + grid_table()
    norm_one, inv_one = layer_norm(x_in)
    act_t, attn_mine, first_mine, norm_one = lax.optimization_barrier(
        (act_t, attn_mine, first_mine, norm_one)
    )
    act_t = act_t.reshape(D, n_all)
    mods_sent = dot(act_t, mod_col, 0, 0) + own_mod_bias.T.reshape(1, 2 * RB)
    mods = (
        exchange(mods_sent[:, None], ALL).reshape(n_shard, 8, RB).transpose(1, 0, 2).reshape(8, 1, D)
    )
    second_mine = after(second_mine, mods)
    attn_halves = (attn_mine, swap(attn_mine, "c"))
    first_halves = (first_mine, swap(first_mine, "c"))
    second_halves = (second_mine, swap(second_mine, "c"))

    target = lax.dynamic_index_in_dim(true_noise, sub, keepdims=False).reshape(SEQ, PATCH)
    head_low = rounded(head_b)
    h_one = (norm_one * (1.0 + mods[1]) + mods[0]).astype(BF)
    own_half = (core, 1 - core)

    def attn_bias(row, which):
        rows = vec_f[row].reshape(2, 2, quarter)
        return lax.dynamic_index_in_dim(rows, which, axis=1, keepdims=False)

    qkv = []
    for weight, which in zip(attn_halves, own_half):
        bias = jnp.stack(
            [attn_bias(11, which), jnp.zeros((2, quarter), F32), attn_bias(12, which)], axis=1
        )
        qkv.append((dot(h_one, weight[:, : 3 * half], 1, 0) + bias.reshape(3 * half)).astype(BF))
    attended = attend(qkv)
    attn_out = vec_f[13]
    for weight, att in zip(attn_halves, attended):
        attn_out = attn_out + dot(att, weight[:, 3 * half :], 1, 1)
    x_one = x_in + mods[2] * attn_out
    norm_two, inv_two = layer_norm(x_one)
    h_two = (norm_two * (1.0 + mods[4]) + mods[3]).astype(BF)
    pre_mlp = []
    act_mlp = []
    mlp_out = vec_f[18]
    for first, second, which in zip(first_halves, second_halves, own_half):
        bias = lax.dynamic_slice_in_dim(vec_f[14:18], which * half, half, axis=1).reshape(wide)
        pre = dot(h_two, first, 1, 0) + bias
        act = gelu_tanh(pre).astype(BF)
        pre_mlp.append(pre)
        act_mlp.append(act)
        mlp_out = mlp_out + dot(act, second, 1, 1)
    x_two = x_one + mods[5] * mlp_out
    norm_fin, inv_fin = layer_norm(x_two)
    y_low = (norm_fin * (1.0 + mods[7]) + mods[6]).astype(BF)
    pred_error = dot(y_low, io_low[PATCH:], 1, 1) + head_low - target.astype(F32)
    loss_own = jnp.sum(pred_error * pred_error)

    d_pred = pred_error * (2.0 / count_all)
    d_pred_low = d_pred.astype(BF)
    grad_head = dot(d_pred_low, y_low, 0, 0)
    grad_hb = jnp.sum(d_pred, axis=0)
    d_y = dot(d_pred_low, io_low[PATCH:], 1, 0)
    d_shift_fin = jnp.sum(d_y, axis=0)
    d_scale_fin = jnp.sum(d_y * norm_fin, axis=0)
    d_two = norm_back(d_y * (1.0 + mods[7]), norm_fin, inv_fin)
    d_gate_two = jnp.sum(d_two * mlp_out, axis=0)
    d_mlp = mods[5] * d_two
    d_mlp_low = d_mlp.astype(BF)
    grad_bfc = jnp.sum(d_mlp, axis=0)
    second_sum = chip_sum([dot(d_mlp_low, act, 0, 0).astype(BF) for act in act_mlp])
    second_z = lax.psum_scatter(second_sum, "z", scatter_dimension=0, tiled=True).reshape(
        2 * n_x, RB, wide
    )
    d_pre_low = []
    hid_bias = []
    d_h_two = 0.0
    d_acts = [dot(d_mlp_low, second, 1, 0) for second in second_halves]
    d_acts = lax.optimization_barrier(tuple(d_acts) + (second_sum,))[:2]
    for pre, first, d_act in zip(pre_mlp, first_halves, d_acts):
        d_pre = jax.vjp(gelu_tanh, pre)[1](d_act)[0]
        hid_bias.append(jnp.sum(d_pre, axis=0).reshape(4, half))
        d_pre_low.append(d_pre.astype(BF))
        d_h_two = d_h_two + dot(d_pre_low[-1], first, 1, 1)
    first_sum = chip_sum([dot(h_two, d, 0, 0).astype(BF) for d in d_pre_low])
    first_parts = first_sum.reshape(n_z, 2, n_x * RB, wide)

    def first_piece(r):
        where = lax.rem(y_at + r, 4)
        return lax.dynamic_slice(
            first_parts, (0, where // 2, 0, where % 2 * D), (n_z, 1, n_x * RB, D)
        )

    first_step = reduce_first(first_piece, ("yh", "yl"))
    grad_bhid = in_order(core, hid_bias[0], hid_bias[1], 1)
    d_shift_two = jnp.sum(d_h_two, axis=0)
    d_scale_two = jnp.sum(d_h_two * norm_two, axis=0)
    d_one = d_two + norm_back(d_h_two * (1.0 + mods[4]), norm_two, inv_two)
    d_gate_one = jnp.sum(d_one * attn_out, axis=0)
    d_attn = mods[2] * d_one
    d_attn_low = after(d_attn.astype(BF), first_sum)
    grad_bout = jnp.sum(d_attn, axis=0)
    d_att = [dot(d_attn_low, weight[:, 3 * half :], 1, 0).astype(BF) for weight in attn_halves]
    d_proj = attend_back(qkv, lax.optimization_barrier(tuple(d_att) + tuple(first_step))[:2])
    first_y = reduce_rest(first_piece, ("yh", "yl"), first_step).astype(BF)
    attn_sum = chip_sum(
        [
            jnp.concatenate(
                [dot(h_one, d, 0, 0).astype(BF), dot(d_attn_low, att, 0, 0).astype(BF)], axis=1
            )
            for d, att in zip(d_proj, attended)
        ]
    )
    attn_parts = attn_sum.reshape(2 * n_z, n_x, RB, wide)

    def attn_piece(r):
        return lax.dynamic_slice_in_dim(attn_parts, lax.rem(x_at + r, n_x), 1, axis=1)

    attn_step = reduce_first(attn_piece, "x")
    d_h_one = sum(
        dot(d, weight[:, : 3 * half], 1, 1) for d, weight in zip(d_proj, attn_halves)
    )
    first_back = exchange(
        after(first_y.reshape(n_z * n_x, RB, D), attn_sum), ("z", "x")
    )
    second_back = exchange(
        jnp.stack([second_z[..., :D], second_z[..., D:]], axis=1).reshape(4 * n_x, RB, D), PLANE
    )
    qv_bias = [
        jnp.sum(d.astype(F32), axis=0).reshape(2, 3, quarter)[:, ::2].transpose(1, 0, 2)[:, :, None]
        for d in d_proj
    ]
    attn_x = reduce_rest(attn_piece, "x", attn_step).astype(BF).reshape(2 * n_z, RB, wide)
    attn_back = exchange(
        jnp.stack([split_y(attn_x, 0), split_y(attn_x, 1)], axis=1).reshape(4 * n_z, RB, D),
        ("z", "yh", "yl"),
    )
    grad_bqv = in_order(core, qv_bias[0], qv_bias[1], 2).reshape(2, D)
    d_shift_one = jnp.sum(d_h_one, axis=0)
    d_scale_one = jnp.sum(d_h_one * norm_one, axis=0)
    d_in = d_one + norm_back(d_h_one * (1.0 + mods[1]), norm_one, inv_one)
    grad_patch = dot(patch_vals, d_in.astype(BF), 0, 0)
    grad_bpatch = jnp.sum(d_in, axis=0)
    d_mods = jnp.stack(
        [
            d_shift_one,
            d_scale_one,
            d_gate_one,
            d_shift_two,
            d_scale_two,
            d_gate_two,
            d_shift_fin,
            d_scale_fin,
        ]
    )

    lanes = 128
    tiles = 2 * D // lanes
    dmod_sent = jnp.broadcast_to(
        d_mods.astype(BF).reshape(1, 4, tiles, lanes), (n_shard, 4, tiles, lanes)
    ).reshape(n_all, tiles, lanes)
    dmod_all = exchange(dmod_sent, ALL)
    mod_sub = lax.dynamic_slice_in_dim(mod_own, 2 * sub, 2, axis=0)
    act_rows = lax.dynamic_slice_in_dim(act_t, shard * RB, RB, axis=0)
    dmod_all = dmod_all.reshape(n_all, 2 * D)
    grad_mod = dot(act_rows, dmod_all, 1, 0).reshape(RB, 2, D).transpose(1, 0, 2)
    d_act = dot(mod_sub.transpose(1, 0, 2).reshape(RB, 2 * D), dmod_all, 1, 1)
    d_act = d_act + swap(d_act, "c")
    d_act = d_act + swap(d_act, "yl")
    d_act = lax.dynamic_slice_in_dim(d_act, sub * vec_cols, vec_cols, axis=0)
    d_cond = jax.vjp(jax.nn.silu, cond_t)[1](d_act)[0]
    grad_table = dot(onehot.astype(F32), d_cond, 0, 1, HIGH)
    grad_bt_two = jnp.sum(d_cond, axis=1)
    d_cond_low = d_cond.astype(BF)
    d_cond_t = to_all(d_cond_low, ALL).reshape(D, n_all)
    d_hidden = dot(temb_low[:, FREQ:], d_cond_t, 1, 0)
    d_pre_time = jax.vjp(jax.nn.silu, pre_t)[1](d_hidden)[0]
    grad_bt_one = lax.dynamic_slice_in_dim(
        jnp.sum(d_pre_time, axis=1), sub * vec_cols, vec_cols, axis=0
    )
    grad_temb = jnp.concatenate(
        [dot(d_pre_time.astype(BF), freq_t, 1, 1), dot(hid_t, d_cond_t, 1, 1)], axis=1
    )

    small = jnp.concatenate(
        [
            grad_bpatch[None],
            d_mods,
            grad_bqv,
            grad_bout[None],
            grad_bhid,
            grad_bfc[None],
            grad_patch,
            grad_head,
        ],
        axis=0,
    )
    n_small = small.shape[0]
    small_sent = jnp.pad(small, ((0, lanes - n_small), (0, 0))).T.reshape(n_all, vec_cols, lanes)
    small_own = jnp.sum(exchange(small_sent, ALL), axis=0).T
    vec_s = jnp.concatenate(
        [small_own[:1], grad_bt_one[None], grad_bt_two[None], small_own[1:17]], axis=0
    )
    io_s = small_own[17:n_small].reshape(2, PATCH, vec_cols)

    mod_c = in_order(core, grad_mod, swap(grad_mod, "c"), 0)
    mod_s = in_order(yl, mod_c, swap(mod_c, "yl"), 0)
    attn_q = jnp.sum(attn_back.astype(F32), axis=0)
    mlp_q = jnp.stack(
        [jnp.sum(first_back.astype(F32), axis=0), jnp.sum(second_back.astype(F32), axis=0)]
    )
    grads_square = jnp.sum(attn_q * attn_q) + jnp.sum(mlp_q * mlp_q)
    attn_q = attn_q.reshape(RB, 4, quarter).transpose(1, 0, 2)
    attn_s = in_order(core, attn_q, swap(attn_q, "c"), 2)
    mlp_s = (
        in_order(yl, mlp_q, swap(mlp_q, "yl"), 2)
        .reshape(2, RB, 4, half)
        .transpose(0, 2, 1, 3)
        .reshape(8, RB, half)
    )

    local_square = (
        grads_square
        + 0.25 * (jnp.sum(mod_s * mod_s) + jnp.sum(grad_temb * grad_temb))
        + jnp.sum(grad_table * grad_table)
        + jnp.sum(io_s * io_s)
        + jnp.sum(vec_s * vec_s)
    )
    sums = jnp.concatenate([local_square[None], loss_own[None], grad_hb])
    sums = jnp.pad(sums, (0, 128 - sums.shape[0]))
    sums = jnp.sum(to_all(sums[None], ALL), axis=0)[0]
    loss = sums[1] / count_all
    head_all = sums[2 : 2 + PATCH]
    grad_norm = jnp.sqrt(sums[0] + jnp.sum(head_all * head_all))
    factor = jnp.minimum(1.0, CLIP_NORM / (grad_norm + 1e-06))

    attn_moment = MOMENT_DECAY * attn_mom + factor * attn_s
    mlp_moment = MOMENT_DECAY * mlp_mom + factor * mlp_s
    mod_moment = MOMENT_DECAY * mod_mom + factor * mod_s
    temb_moment = MOMENT_DECAY * temb_mom + factor * grad_temb
    gram_attn = jnp.einsum("bij,bkj->bik", attn_moment, attn_moment, precision=HIGH)
    gram_mlp = jnp.einsum("bij,bkj->bik", mlp_moment, mlp_moment, precision=HIGH)
    gram_mod = jnp.einsum("bij,bkj->bik", mod_moment, mod_moment, precision=HIGH)
    temb_left, temb_right = temb_moment[:, :FREQ], temb_moment[:, FREQ:]
    gram_left = dot(temb_left, temb_left, 1, 1, HIGH)[None]
    gram_right = dot(temb_right, temb_right, 1, 1, HIGH)[None]
    gram_attn = gram_attn + swap(gram_attn, "yl")
    gram_mlp = gram_mlp + swap(gram_mlp, "c")
    maps = newton_maps(
        jnp.concatenate(
            [gram_attn, gram_left, gram_right, jnp.zeros((2, RB, RB), F32), gram_mlp, gram_mod]
        )
    )
    n_attn = 4 * RB
    attn_ortho = dot(
        maps[0, :n_attn, :n_attn], attn_moment.reshape(n_attn, half), 1, 0, HIGH
    ).reshape(attn_moment.shape)
    left_ortho = dot(
        maps[0, n_attn : n_attn + RB, n_attn : n_attn + RB], temb_left, 1, 0, HIGH
    )
    right_ortho = dot(
        maps[0, n_attn + RB : n_attn + 2 * RB, n_attn + RB : n_attn + 2 * RB],
        temb_right,
        1,
        0,
        HIGH,
    )
    mlp_ortho = dot(maps[1], mlp_moment.reshape(8 * RB, half), 1, 0, HIGH).reshape(
        mlp_moment.shape
    )
    mod_ortho = dot(maps[2], mod_moment.reshape(8 * RB, D), 1, 0, HIGH).reshape(mod_moment.shape)
    attn_new = attn_w - LR_MUON * attn_ortho
    mlp_new = mlp_w - LR_MUON * mlp_ortho
    mod_new = mod_w - LR_MUON * mod_ortho
    temb_new = temb_w - LR_MUON * jnp.concatenate([left_ortho, right_ortho], axis=1)
    table_new, table_first_new, table_second_new = adam(
        label_table, table_first, table_second, factor * grad_table, 0.3
    )
    io_rates = jnp.array([0.1, 0.01], F32).reshape(2, 1, 1)
    io_new, io_first_new, io_second_new = adam(io_w, io_first, io_second, factor * io_s, io_rates)
    vec_new, vec_first_new, vec_second_new = adam(
        vec_w, vec_first, vec_second, factor * vec_s, 0.05
    )
    headb_new, headb_first_new, headb_second_new = adam(
        head_b, headb_first, headb_second, factor * head_all, 0.05
    )
    return (
        loss,
        grad_norm,
        attn_new,
        attn_moment,
        attn_new.astype(BF),
        mlp_new,
        mlp_moment,
        mlp_new.astype(BF),
        mod_new,
        mod_moment,
        mod_new.astype(BF),
        temb_new,
        temb_moment,
        table_new,
        table_first_new,
        table_second_new,
        table_new.astype(BF),
        io_new,
        io_first_new,
        io_second_new,
        vec_new,
        vec_first_new,
        vec_second_new,
        headb_new,
        headb_first_new,
        headb_second_new,
    )


def chip_sum(halves):
    mine, other = halves
    return (mine.astype(F32) + swap(other, "c").astype(F32)).astype(BF)


def solution(mesh):
    fine = Mesh(mesh.devices.reshape(SHARD_SIZES + (2, 2)), ALL)
    lat = P(SHARD, None)
    one = P(SHARD)
    attn = P(None, SHARD, "yl")
    mlp = P(None, SHARD, "c")
    mod = P(None, SHARD, None)
    temb = P(SHARD, None)
    flat = P(None, ALL)
    io = P(None, None, ALL)
    rep = P()
    return jax.shard_map(
        on_device,
        mesh=fine,
        in_specs=(lat, lat, one, one, attn, attn, mlp, mlp, mod, mod, temb, temb)
        + (flat,) * 3
        + (io,) * 3
        + (flat,) * 3
        + (rep,) * 3,
        out_specs=(rep, rep)
        + (attn,) * 3
        + (mlp,) * 3
        + (mod,) * 3
        + (temb,) * 2
        + (flat,) * 4
        + (io,) * 3
        + (flat,) * 3
        + (rep,) * 3,
        check_vma=False,
    )
```

```python
import functools
import math

import jax
import jax.numpy as jnp
from jax import lax
from jax.experimental import pallas as pl
from jax.experimental.pallas import tpu as pltpu
from jax.sharding import Mesh
from jax.sharding import PartitionSpec as P

D = 1024
HDIM = 64
FREQ = 256
NCLS = 1000
PATCH = 16
GRID = 16
SEQ = 256
RB = 16
NS_STEPS = 5
STEP = 10
SHARD_SIZES = (8, 2, 4)
INTERPRET = False

HIGH = lax.Precision.HIGHEST
NS_A = 3.4445
NS_B = -4.775
NS_C = 2.0315
CLIP_NORM = 0.01
LR_MUON = 0.5
MOMENT_DECAY = 0.5
BETA_ONE = 0.5
BETA_TWO = 0.5
ADAM_EPS = 1e-08
LN_EPS = 1e-06

BF = jnp.bfloat16
F32 = jnp.float32

SHARD = ("z", "yh", "x")
PLANE = ("yh", "x", "yl")
ALL = ("z", "yh", "x", "yl", "c")


def dot(lhs, rhs, lhs_dim, rhs_dim, precision=None):
    return lax.dot_general(
        lhs,
        rhs,
        (((lhs_dim,), (rhs_dim,)), ((), ())),
        precision=precision,
        preferred_element_type=F32,
    )


def rounded(v):
    return lax.reduce_precision(v.astype(F32), 8, 7)


def exchange(v, axes):
    return lax.all_to_all(v, axes, 0, 0)


def to_all(v, axes):
    return exchange(jnp.broadcast_to(v[None], (lax.axis_size(axes),) + v.shape), axes)


def after(v, *others):
    return lax.optimization_barrier((v,) + others)[0]


def swap(v, axis):
    return lax.ppermute(v, axis, [(0, 1), (1, 0)])


def all_after(values, *others):
    return lax.optimization_barrier(tuple(values) + others)[: len(values)]


def added(one, two):
    return (one.astype(F32) + two.astype(F32)).astype(BF)


def in_order(index, mine, other, axis):
    return jnp.where(
        index == 0,
        jnp.concatenate([mine, other], axis=axis),
        jnp.concatenate([other, mine], axis=axis),
    )


def join_y(low, high):
    cut = 3 * low.shape[-1] // 4
    return jnp.concatenate(
        [low[..., :cut], high[..., :cut], low[..., cut:], high[..., cut:]], axis=-1
    )


def split_y(v, side):
    width = v.shape[-1] // 8
    return jnp.concatenate(
        [
            v[..., 3 * side * width : 3 * (side + 1) * width],
            v[..., (6 + side) * width : (7 + side) * width],
        ],
        axis=-1,
    )


def grid_table():
    quarter = D // 4
    rates = jnp.exp(-math.log(10000.0) * jnp.arange(quarter, dtype=F32) / quarter)
    phases = jnp.arange(GRID).astype(F32)[:, None] * rates[None, :]
    sines, cosines = jnp.sin(phases), jnp.cos(phases)
    full = (GRID, GRID, quarter)
    return jnp.concatenate(
        [
            jnp.broadcast_to(sines[None], full),
            jnp.broadcast_to(cosines[None], full),
            jnp.broadcast_to(sines[:, None], full),
            jnp.broadcast_to(cosines[:, None], full),
        ],
        axis=2,
    ).reshape(SEQ, D)


def layer_norm(values):
    center = jnp.mean(values, axis=-1, keepdims=True)
    shifted = values - center
    inv_std = lax.rsqrt(jnp.mean(shifted * shifted, axis=-1, keepdims=True) + LN_EPS)
    return (shifted * inv_std, inv_std)


def norm_back(grad_norm, normed, inv_std):
    return inv_std * (
        grad_norm
        - jnp.mean(grad_norm, axis=-1, keepdims=True)
        - normed * jnp.mean(grad_norm * normed, axis=-1, keepdims=True)
    )


def gelu_tanh(values):
    return jax.nn.gelu(values, approximate=True)


def newton_kernel(gram_ref, norm_ref, out_ref):
    size = gram_ref.shape[-1]
    rows = lax.broadcasted_iota(jnp.int32, (size, size), 0)
    cols = lax.broadcasted_iota(jnp.int32, (size, size), 1)
    eye = (rows == cols).astype(F32)
    groups = gram_ref.shape[0]
    inv = [1.0 / norm_ref[g] for g in range(groups)]
    quad = [gram_ref[g] * (inv[g] * inv[g]) for g in range(groups)]
    total = [None] * groups

    def mul(a, b):
        return jnp.dot(a, b, precision=HIGH, preferred_element_type=F32)

    for turn in range(NS_STEPS):
        poly = [NS_A * eye + NS_B * q + NS_C * mul(q, q) for q in quad]
        total = [p if turn == 0 else mul(p, t) for p, t in zip(poly, total)]
        if turn < NS_STEPS - 1:
            half = [mul(p, q) for p, q in zip(poly, quad)]
            quad = [mul(h, p) for h, p in zip(half, poly)]
    for g in range(groups):
        out_ref[g] = total[g] * inv[g]


def newton_maps(grams):
    size = 8 * RB
    groups = grams.shape[0] // 8
    norms = jnp.sqrt(jnp.einsum("bii->b", grams)) + 1e-07
    place = jnp.arange(size) // RB
    same = (place[:, None] == place[None, :])[None]
    tiled = jnp.tile(grams.reshape(groups, size, RB), (1, 1, 8))
    blocks = jnp.where(same, tiled, 0.0)
    norm_rows = jnp.broadcast_to(
        jnp.repeat(norms, RB).reshape(groups, size, 1), (groups, size, size)
    )
    return pl.pallas_call(
        newton_kernel,
        out_shape=jax.ShapeDtypeStruct((groups, size, size), F32),
        interpret=INTERPRET,
    )(blocks, norm_rows)


def adam(weight, first_old, second_old, grad_in, step_rate):
    first_new = BETA_ONE * first_old + (1.0 - BETA_ONE) * grad_in
    second_new = BETA_TWO * second_old + (1.0 - BETA_TWO) * grad_in * grad_in
    fix_one = 1.0 - BETA_ONE**STEP
    fix_two = 1.0 - BETA_TWO**STEP
    new_weight = weight - step_rate * (first_new / fix_one) / (
        jnp.sqrt(second_new / fix_two) + ADAM_EPS
    )
    return (new_weight, first_new, second_new)


def across_rows(lhs, rhs):
    return dot(lhs, rhs, 1, 1)


def head_probs(q, k, side):
    lane = lax.broadcasted_iota(jnp.int32, (1, 2 * HDIM), 1)
    mask = (lane // HDIM == side).astype(F32)
    scores = across_rows((q.astype(F32) * mask).astype(BF), k) * (1.0 / math.sqrt(HDIM))
    grown = jnp.exp(scores - jnp.max(scores, axis=-1, keepdims=True))
    return grown / jnp.sum(grown, axis=-1, keepdims=True), mask


def attend_kernel(*refs):
    for half in range(2):
        q, k, v = (r[...] for r in refs[3 * half : 3 * half + 3])
        out = 0.0
        for side in range(2):
            probs, mask = head_probs(q, k, side)
            out = out + mask * dot(probs.astype(BF), v, 1, 0)
        refs[6 + half][...] = out.astype(BF)


def attend_back_kernel(*refs):
    block = pl.program_id(0)
    per = pl.num_programs(0) // 2
    for half in range(2):
        q, k, v, d_att = (r[...] for r in refs[4 * half : 4 * half + 4])
        d_q, d_k, d_v = 0.0, 0.0, 0.0
        for side in range(2):
            probs, mask = head_probs(q, k, side)
            d_probs = across_rows((d_att.astype(F32) * mask).astype(BF), v)
            d_v = d_v + mask * dot(probs.astype(BF), d_att, 0, 0)
            row_dot = jnp.sum(d_probs * probs, axis=-1, keepdims=True)
            d_raw = (probs * (d_probs - row_dot) * (1.0 / math.sqrt(HDIM))).astype(BF)
            d_q = d_q + mask * dot(d_raw, k, 1, 0)
            d_k = d_k + mask * dot(d_raw, q, 0, 0)
        for at, value in enumerate((d_q, d_k, d_v)):
            where = pl.multiple_of(qkv_block(block, at, per) * 2 * HDIM, 2 * HDIM)
            refs[8 + half][:, pl.ds(where, 2 * HDIM)] = value.astype(BF)


def qkv_block(j, at, per):
    return (j // per) * 3 * per + at * per + j % per


def columns(at=None, per=1):
    if at is None:
        return pl.BlockSpec((SEQ, 2 * HDIM), lambda j: (0, j))
    return pl.BlockSpec((SEQ, 2 * HDIM), lambda j: (0, qkv_block(j, at, per)))


def attend(qkv):
    width = qkv[0].shape[1] // 3
    groups = width // (2 * HDIM)
    return pl.pallas_call(
        attend_kernel,
        grid=(groups,),
        in_specs=[columns(at, groups // 2) for at in range(3)] * 2,
        out_specs=[columns()] * 2,
        out_shape=[jax.ShapeDtypeStruct((SEQ, width), BF)] * 2,
        cost_estimate=pl.CostEstimate(
            flops=16 * SEQ * SEQ * width, bytes_accessed=16 * SEQ * width, transcendentals=8 * SEQ * SEQ
        ),
        interpret=INTERPRET,
    )(*(qkv[0],) * 3, *(qkv[1],) * 3)


def attend_back(qkv, d_att):
    width = qkv[0].shape[1] // 3
    groups = width // (2 * HDIM)
    whole = pl.BlockSpec((SEQ, 3 * width), lambda j: (0, 0))
    return pl.pallas_call(
        attend_back_kernel,
        grid=(groups,),
        in_specs=([columns(at, groups // 2) for at in range(3)] + [columns()]) * 2,
        out_specs=[whole] * 2,
        out_shape=[jax.ShapeDtypeStruct((SEQ, 3 * width), BF)] * 2,
        cost_estimate=pl.CostEstimate(
            flops=40 * SEQ * SEQ * width, bytes_accessed=28 * SEQ * width, transcendentals=8 * SEQ * SEQ
        ),
        interpret=INTERPRET,
    )(*(qkv[0],) * 3, d_att[0], *(qkv[1],) * 3, d_att[1])


def on_device(
    noisy_patches,
    true_noise,
    timesteps,
    labels,
    attn_w,
    attn_mom,
    mlp_w,
    mlp_mom,
    mod_w,
    mod_mom,
    temb_w,
    temb_mom,
    label_table,
    table_first,
    table_second,
    io_w,
    io_first,
    io_second,
    vec_w,
    vec_first,
    vec_second,
    head_b,
    headb_first,
    headb_second,
):
    n_shard = lax.axis_size(SHARD)
    n_all = lax.axis_size(ALL)
    count_all = n_all * SEQ * PATCH
    yl, core = lax.axis_index("yl"), lax.axis_index("c")
    sub = 2 * yl + core
    shard = lax.axis_index(SHARD)
    half = D // 2
    quarter = D // 4
    wide = 4 * half

    n_x = lax.axis_size("x")
    attn_low = lax.dynamic_slice_in_dim(attn_w, core * quarter, quarter, axis=2).astype(BF)
    attn_own = attn_low.transpose(1, 0, 2).reshape(RB, 4 * quarter)
    mlp_low = (
        lax.dynamic_slice_in_dim(mlp_w.reshape(2, 4, RB, half), 2 * yl, 2, axis=1)
        .astype(BF)
        .transpose(0, 2, 1, 3)
        .reshape(2, RB, D)
    )
    plane_rows = to_all(jnp.concatenate([attn_own, mlp_low[0], mlp_low[1]], axis=1), PLANE)
    plane_rows = plane_rows.reshape(2 * n_x, 2, RB, 3 * D)
    low, high = plane_rows[:, 0], plane_rows[:, 1]
    attn_mine = lax.all_gather(
        join_y(low[..., :D], high[..., :D]).reshape(-1, wide), "z", axis=0, tiled=True
    )
    mlp_mine = lax.all_gather(
        jnp.concatenate(
            [low[..., D : 2 * D], high[..., D : 2 * D], low[..., 2 * D :], high[..., 2 * D :]],
            axis=-1,
        ).reshape(-1, 2 * wide),
        "z",
        axis=0,
        tiled=True,
    )

    label_own = lax.dynamic_index_in_dim(labels, sub, keepdims=False)
    time_own = lax.dynamic_index_in_dim(timesteps, sub, keepdims=False)
    vec_cols = vec_w.shape[1]
    lanes_io = vec_w.shape[0]
    lanes_int = lanes_io + 2 * PATCH
    lanes_mod = 64
    lanes_all = 128
    ints = jnp.stack([label_own // 32, label_own % 32, time_own // 32, time_own % 32])
    common = jnp.concatenate(
        [
            vec_w.T.astype(BF),
            io_w.reshape(2 * PATCH, vec_cols).T.astype(BF),
            jnp.broadcast_to(ints.astype(BF)[None], (vec_cols, 4)),
            jnp.zeros((vec_cols, lanes_mod - lanes_int - 4), BF),
        ],
        axis=1,
    )
    mod_own = mod_w.astype(BF)
    mod_cols = (
        lax.dynamic_slice_in_dim(mod_own, sub * 4, 4, axis=1)
        .reshape(4, 2, 4, n_shard, RB)
        .transpose(3, 0, 2, 1, 4)
        .reshape(n_all, 4, 2 * RB)
    )
    sent = jnp.concatenate(
        [
            jnp.broadcast_to(common[None], (n_all,) + common.shape),
            mod_cols,
            jnp.zeros((n_all, 4, lanes_all - lanes_mod - 2 * RB), BF),
        ],
        axis=2,
    )
    got = exchange(sent, ALL)
    marks = got[:, 0, lanes_int : lanes_int + 4].astype(F32)
    labels_all = (marks[:, 0] * 32.0 + marks[:, 1]).astype(jnp.int32)
    times_all = marks[:, 2] * 32.0 + marks[:, 3]
    by_feature = got.reshape(D, lanes_all)
    by_row = by_feature[:, :lanes_int].astype(F32).T
    vec_f = by_row[:lanes_io]
    io_low = by_row[lanes_io:lanes_int].astype(BF)
    mod_col = by_feature[:, lanes_mod : lanes_mod + 2 * RB]
    own_features = lax.dynamic_slice_in_dim(by_feature, shard * RB, RB, axis=0)[
        :, :lanes_io
    ].astype(F32)
    own_mod_bias = lax.dynamic_slice_in_dim(own_features, 3 + 2 * sub, 2, axis=1)

    rates = jnp.exp(-math.log(10000.0) * jnp.arange(FREQ // 2, dtype=F32) / (FREQ // 2))
    phases = rates[:, None] * times_all[None, :]
    freq_t = jnp.concatenate([jnp.cos(phases), jnp.sin(phases)], axis=0).astype(BF)
    temb_low = temb_w.astype(BF)
    pre_t = dot(temb_low[:, :FREQ], freq_t, 1, 0) + own_features[:, 1:2]
    hid_t = jax.nn.silu(pre_t).astype(BF)
    temb_cols = lax.dynamic_slice_in_dim(
        temb_low[:, FREQ:].reshape(RB, n_shard, 4, vec_cols), sub, 1, axis=2
    ).reshape(RB, n_shard * vec_cols)
    cond_parts = dot(temb_cols, hid_t, 0, 0)
    cond_parts = exchange(
        cond_parts.reshape(n_shard, vec_cols, n_all), SHARD
    )
    onehot = (labels_all[:, None] == jnp.arange(NCLS)[None, :]).astype(BF)
    label_rows = dot(label_table.astype(BF), onehot, 0, 1)
    cond_t = jnp.sum(cond_parts, axis=0) + label_rows + rounded(vec_w[2])[:, None]
    act_own = jax.nn.silu(cond_t).astype(BF)
    act_t = to_all(act_own, ALL)
    patch_vals = lax.dynamic_index_in_dim(noisy_patches, sub, keepdims=False).reshape(SEQ, PATCH)
    x_in = dot(patch_vals, io_low[:PATCH], 1, 0) + vec_f[0] + grid_table()
    norm_one, inv_one = layer_norm(x_in)
    act_t, attn_mine, norm_one = lax.optimization_barrier((act_t, attn_mine, norm_one))
    attn_halves = (attn_mine, swap(attn_mine, "c"))
    act_t = act_t.reshape(D, n_all)
    mods_sent = dot(act_t, mod_col, 0, 0) + own_mod_bias.T.reshape(1, 2 * RB)
    mods = (
        exchange(mods_sent[:, None], ALL).reshape(n_shard, 8, RB).transpose(1, 0, 2).reshape(8, 1, D)
    )
    target = lax.dynamic_index_in_dim(true_noise, sub, keepdims=False).reshape(SEQ, PATCH)
    head_low = rounded(head_b)
    h_one = (norm_one * (1.0 + mods[1]) + mods[0]).astype(BF)
    own_half = (core, 1 - core)

    def attn_bias(row, which):
        rows = vec_f[row].reshape(2, 2, quarter)
        return lax.dynamic_index_in_dim(rows, which, axis=1, keepdims=False)

    qkv = []
    for weight, which in zip(attn_halves, own_half):
        bias = jnp.stack(
            [attn_bias(11, which), jnp.zeros((2, quarter), F32), attn_bias(12, which)], axis=1
        )
        qkv.append((dot(h_one, weight[:, : 3 * half], 1, 0) + bias.reshape(3 * half)).astype(BF))
    attended = attend(qkv)
    mlp_mine = after(mlp_mine, attended[0])
    mlp_halves = (mlp_mine, swap(mlp_mine, "c"))
    first_halves = [m[:, :wide] for m in mlp_halves]
    second_halves = [m[:, wide:] for m in mlp_halves]
    attn_out = vec_f[13]
    for weight, att in zip(attn_halves, attended):
        attn_out = attn_out + dot(att, weight[:, 3 * half :], 1, 1)
    x_one = x_in + mods[2] * attn_out
    norm_two, inv_two = layer_norm(x_one)
    h_two = (norm_two * (1.0 + mods[4]) + mods[3]).astype(BF)
    pre_mlp = []
    act_mlp = []
    mlp_out = vec_f[18]
    for first, second, which in zip(first_halves, second_halves, own_half):
        bias = lax.dynamic_slice_in_dim(vec_f[14:18], which * half, half, axis=1).reshape(wide)
        pre = dot(h_two, first, 1, 0) + bias
        act = gelu_tanh(pre).astype(BF)
        pre_mlp.append(pre)
        act_mlp.append(act)
        mlp_out = mlp_out + dot(act, second, 1, 1)
    x_two = x_one + mods[5] * mlp_out
    norm_fin, inv_fin = layer_norm(x_two)
    y_low = (norm_fin * (1.0 + mods[7]) + mods[6]).astype(BF)
    pred_error = dot(y_low, io_low[PATCH:], 1, 1) + head_low - target.astype(F32)
    loss_own = jnp.sum(pred_error * pred_error)

    d_pred = pred_error * (2.0 / count_all)
    d_pred_low = d_pred.astype(BF)
    grad_head = dot(d_pred_low, y_low, 0, 0)
    grad_hb = jnp.sum(d_pred, axis=0)
    d_y = dot(d_pred_low, io_low[PATCH:], 1, 0)
    d_shift_fin = jnp.sum(d_y, axis=0)
    d_scale_fin = jnp.sum(d_y * norm_fin, axis=0)
    d_two = norm_back(d_y * (1.0 + mods[7]), norm_fin, inv_fin)
    d_gate_two = jnp.sum(d_two * mlp_out, axis=0)
    d_mlp = mods[5] * d_two
    d_mlp_low = d_mlp.astype(BF)
    grad_bfc = jnp.sum(d_mlp, axis=0)
    d_acts = [dot(d_mlp_low, second, 1, 0) for second in second_halves]
    second_sum = chip_sum([dot(d_mlp_low, act, 0, 0).astype(BF) for act in act_mlp], *d_acts)
    second_z = lax.psum_scatter(second_sum, "z", scatter_dimension=0, tiled=True)
    d_pre_low = []
    hid_bias = []
    d_h_two = 0.0
    d_acts = lax.optimization_barrier(tuple(d_acts) + (second_sum,))[:2]
    for pre, first, d_act in zip(pre_mlp, first_halves, d_acts):
        d_pre = jax.vjp(gelu_tanh, pre)[1](d_act)[0]
        hid_bias.append(jnp.sum(d_pre, axis=0).reshape(4, half))
        d_pre_low.append(d_pre.astype(BF))
        d_h_two = d_h_two + dot(d_pre_low[-1], first, 1, 1)
    first_sum = chip_sum([dot(h_two, d, 0, 0).astype(BF) for d in d_pre_low])
    first_z = lax.psum_scatter(first_sum, "z", scatter_dimension=0, tiled=True)
    grad_bhid = in_order(core, hid_bias[0], hid_bias[1], 1)
    d_shift_two = jnp.sum(d_h_two, axis=0)
    d_scale_two = jnp.sum(d_h_two * norm_two, axis=0)
    d_one = d_two + norm_back(d_h_two * (1.0 + mods[4]), norm_two, inv_two)
    d_gate_one = jnp.sum(d_one * attn_out, axis=0)
    d_attn = mods[2] * d_one
    d_attn_low = after(d_attn.astype(BF), first_sum)
    grad_bout = jnp.sum(d_attn, axis=0)
    d_att = [dot(d_attn_low, weight[:, 3 * half :], 1, 0).astype(BF) for weight in attn_halves]
    d_proj = all_after(attend_back(qkv, d_att), second_z)
    d_h_one = sum(
        dot(d, weight[:, : 3 * half], 1, 1) for d, weight in zip(d_proj, attn_halves)
    )
    qv_bias = [
        jnp.sum(d.astype(F32), axis=0).reshape(2, 3, quarter)[:, ::2].transpose(1, 0, 2)[:, :, None]
        for d in d_proj
    ]
    grad_bqv = in_order(core, qv_bias[0], qv_bias[1], 2).reshape(2, D)
    d_shift_one = jnp.sum(d_h_one, axis=0)
    d_scale_one = jnp.sum(d_h_one * norm_one, axis=0)
    d_in = d_one + norm_back(d_h_one * (1.0 + mods[1]), norm_one, inv_one)
    grad_patch = dot(patch_vals, d_in.astype(BF), 0, 0)
    grad_bpatch = jnp.sum(d_in, axis=0)
    d_mods = jnp.stack(
        [
            d_shift_one,
            d_scale_one,
            d_gate_one,
            d_shift_two,
            d_scale_two,
            d_gate_two,
            d_shift_fin,
            d_scale_fin,
        ]
    )

    lanes = 128
    small = jnp.concatenate(
        [
            grad_bpatch[None],
            d_mods,
            grad_bqv,
            grad_bout[None],
            grad_bhid,
            grad_bfc[None],
            grad_patch,
            grad_head,
        ],
        axis=0,
    )
    n_small = small.shape[0]
    small = jnp.pad(small, ((0, lanes - n_small), (0, 0))).T.astype(BF)
    tiles = 2 * D // lanes
    dmod_sent = jnp.broadcast_to(
        d_mods.astype(BF).reshape(1, 4, tiles, lanes), (n_shard, 4, tiles, lanes)
    ).reshape(n_all, tiles, lanes)
    dmod_all = exchange(dmod_sent, ALL)
    held = all_after(tuple(d_proj), small)
    grads = [
        jnp.concatenate(
            [dot(h_one, d, 0, 0).astype(BF), dot(d_attn_low, att, 0, 0).astype(BF), small], axis=1
        )
        for d, att in zip(held, attended)
    ]
    attn_sum = after(chip_sum(grads), first_z, dmod_all)
    attn_z = lax.psum_scatter(attn_sum, "z", scatter_dimension=0, tiled=True)

    mod_sub = lax.dynamic_slice_in_dim(mod_own, 2 * sub, 2, axis=0)
    act_rows = lax.dynamic_slice_in_dim(act_t, shard * RB, RB, axis=0)
    dmod_all = dmod_all.reshape(n_all, 2 * D)
    grad_mod = dot(act_rows, dmod_all, 1, 0).reshape(RB, 2, D).transpose(1, 0, 2)
    d_act = dot(mod_sub.transpose(1, 0, 2).reshape(RB, 2 * D), dmod_all, 1, 1)
    d_act = d_act + swap(d_act, "c")
    d_act = d_act + swap(d_act, "yl")
    d_act = lax.dynamic_slice_in_dim(d_act, sub * vec_cols, vec_cols, axis=0)
    d_cond = jax.vjp(jax.nn.silu, cond_t)[1](d_act)[0]
    grad_table = dot(onehot.astype(F32), d_cond, 0, 1, HIGH)
    grad_bt_two = jnp.sum(d_cond, axis=1)
    d_cond_low = d_cond.astype(BF)
    d_cond_t = to_all(d_cond_low, ALL).reshape(D, n_all)
    d_hidden = dot(temb_low[:, FREQ:], d_cond_t, 1, 0)
    d_pre_time = jax.vjp(jax.nn.silu, pre_t)[1](d_hidden)[0]
    grad_bt_one = lax.dynamic_slice_in_dim(
        jnp.sum(d_pre_time, axis=1), sub * vec_cols, vec_cols, axis=0
    )
    grad_temb = jnp.concatenate(
        [dot(d_pre_time.astype(BF), freq_t, 1, 1), dot(hid_t, d_cond_t, 1, 1)], axis=1
    )

    mod_c = in_order(core, grad_mod, swap(grad_mod, "c"), 0)
    mod_s = in_order(yl, mod_c, swap(mod_c, "yl"), 0)
    rows = (2 * n_x, RB, -1)
    attn_z, first_z, second_z = attn_z.reshape(rows), first_z.reshape(rows), second_z.reshape(rows)
    plane_sent = jnp.stack(
        [
            jnp.concatenate(
                [
                    split_y(attn_z[..., :wide], side),
                    first_z[..., side * D : (side + 1) * D],
                    second_z[..., side * D : (side + 1) * D],
                    attn_z[..., wide:],
                ],
                axis=-1,
            )
            for side in range(2)
        ],
        axis=1,
    ).reshape(4 * n_x, RB, 3 * D + lanes)
    plane_own = jnp.sum(exchange(plane_sent, PLANE).astype(F32), axis=0)
    attn_q = plane_own[:, :D]
    mlp_q = jnp.stack([plane_own[:, D : 2 * D], plane_own[:, 2 * D : 3 * D]])
    small_own = lax.dynamic_slice_in_dim(plane_own[:, 3 * D :], sub * vec_cols, vec_cols, axis=0).T
    vec_s = jnp.concatenate(
        [small_own[:1], grad_bt_one[None], grad_bt_two[None], small_own[1:17]], axis=0
    )
    io_s = small_own[17:n_small].reshape(2, PATCH, vec_cols)

    grads_square = jnp.sum(attn_q * attn_q) + jnp.sum(mlp_q * mlp_q)
    attn_q = attn_q.reshape(RB, 4, quarter).transpose(1, 0, 2)
    attn_s = in_order(core, attn_q, swap(attn_q, "c"), 2)
    mlp_s = (
        in_order(yl, mlp_q, swap(mlp_q, "yl"), 2)
        .reshape(2, RB, 4, half)
        .transpose(0, 2, 1, 3)
        .reshape(8, RB, half)
    )

    local_square = (
        grads_square
        + 0.25 * (jnp.sum(mod_s * mod_s) + jnp.sum(grad_temb * grad_temb))
        + jnp.sum(grad_table * grad_table)
        + jnp.sum(io_s * io_s)
        + jnp.sum(vec_s * vec_s)
    )
    sums = jnp.concatenate([local_square[None], loss_own[None], grad_hb])
    sums = jnp.pad(sums, (0, 128 - sums.shape[0]))
    sums = jnp.sum(to_all(sums[None], ALL), axis=0)[0]
    loss = sums[1] / count_all
    head_all = sums[2 : 2 + PATCH]
    grad_norm = jnp.sqrt(sums[0] + jnp.sum(head_all * head_all))
    factor = jnp.minimum(1.0, CLIP_NORM / (grad_norm + 1e-06))

    attn_moment = MOMENT_DECAY * attn_mom + factor * attn_s
    mlp_moment = MOMENT_DECAY * mlp_mom + factor * mlp_s
    mod_moment = MOMENT_DECAY * mod_mom + factor * mod_s
    temb_moment = MOMENT_DECAY * temb_mom + factor * grad_temb
    gram_attn = jnp.einsum("bij,bkj->bik", attn_moment, attn_moment, precision=HIGH)
    gram_mlp = jnp.einsum("bij,bkj->bik", mlp_moment, mlp_moment, precision=HIGH)
    gram_mod = jnp.einsum("bij,bkj->bik", mod_moment, mod_moment, precision=HIGH)
    temb_left, temb_right = temb_moment[:, :FREQ], temb_moment[:, FREQ:]
    gram_left = dot(temb_left, temb_left, 1, 1, HIGH)[None]
    gram_right = dot(temb_right, temb_right, 1, 1, HIGH)[None]
    gram_attn = gram_attn + swap(gram_attn, "yl")
    gram_mlp = gram_mlp + swap(gram_mlp, "c")
    maps = newton_maps(
        jnp.concatenate(
            [gram_attn, gram_left, gram_right, jnp.zeros((2, RB, RB), F32), gram_mlp, gram_mod]
        )
    )
    n_attn = 4 * RB
    attn_ortho = dot(
        maps[0, :n_attn, :n_attn], attn_moment.reshape(n_attn, half), 1, 0, HIGH
    ).reshape(attn_moment.shape)
    left_ortho = dot(
        maps[0, n_attn : n_attn + RB, n_attn : n_attn + RB], temb_left, 1, 0, HIGH
    )
    right_ortho = dot(
        maps[0, n_attn + RB : n_attn + 2 * RB, n_attn + RB : n_attn + 2 * RB],
        temb_right,
        1,
        0,
        HIGH,
    )
    mlp_ortho = dot(maps[1], mlp_moment.reshape(8 * RB, half), 1, 0, HIGH).reshape(
        mlp_moment.shape
    )
    mod_ortho = dot(maps[2], mod_moment.reshape(8 * RB, D), 1, 0, HIGH).reshape(mod_moment.shape)
    attn_new = attn_w - LR_MUON * attn_ortho
    mlp_new = mlp_w - LR_MUON * mlp_ortho
    mod_new = mod_w - LR_MUON * mod_ortho
    temb_new = temb_w - LR_MUON * jnp.concatenate([left_ortho, right_ortho], axis=1)
    table_new, table_first_new, table_second_new = adam(
        label_table, table_first, table_second, factor * grad_table, 0.3
    )
    io_rates = jnp.array([0.1, 0.01], F32).reshape(2, 1, 1)
    io_new, io_first_new, io_second_new = adam(io_w, io_first, io_second, factor * io_s, io_rates)
    vec_new, vec_first_new, vec_second_new = adam(
        vec_w, vec_first, vec_second, factor * vec_s, 0.05
    )
    headb_new, headb_first_new, headb_second_new = adam(
        head_b, headb_first, headb_second, factor * head_all, 0.05
    )
    return (
        loss,
        grad_norm,
        attn_new,
        attn_moment,
        attn_new.astype(BF),
        mlp_new,
        mlp_moment,
        mlp_new.astype(BF),
        mod_new,
        mod_moment,
        mod_new.astype(BF),
        temb_new,
        temb_moment,
        table_new,
        table_first_new,
        table_second_new,
        table_new.astype(BF),
        io_new,
        io_first_new,
        io_second_new,
        vec_new,
        vec_first_new,
        vec_second_new,
        headb_new,
        headb_first_new,
        headb_second_new,
    )


def chip_sum(halves, *between):
    mine, other = halves
    return (mine.astype(F32) + after(swap(other, "c"), *between).astype(F32)).astype(BF)


def solution(mesh):
    fine = Mesh(mesh.devices.reshape(SHARD_SIZES + (2, 2)), ALL)
    lat = P(SHARD, None)
    one = P(SHARD)
    attn = P(None, SHARD, "yl")
    mlp = P(None, SHARD, "c")
    mod = P(None, SHARD, None)
    temb = P(SHARD, None)
    flat = P(None, ALL)
    io = P(None, None, ALL)
    rep = P()
    return jax.shard_map(
        on_device,
        mesh=fine,
        in_specs=(lat, lat, one, one, attn, attn, mlp, mlp, mod, mod, temb, temb)
        + (flat,) * 3
        + (io,) * 3
        + (flat,) * 3
        + (rep,) * 3,
        out_specs=(rep, rep)
        + (attn,) * 3
        + (mlp,) * 3
        + (mod,) * 3
        + (temb,) * 2
        + (flat,) * 4
        + (io,) * 3
        + (flat,) * 3
        + (rep,) * 3,
        check_vma=False,
    )
```

```python
import functools
import math

import jax
import jax.numpy as jnp
from jax import lax
from jax.experimental import pallas as pl
from jax.experimental.pallas import tpu as pltpu
from jax.sharding import Mesh
from jax.sharding import PartitionSpec as P

D = 1024
HDIM = 64
FREQ = 256
NCLS = 1000
PATCH = 16
GRID = 16
SEQ = 256
RB = 16
NS_STEPS = 5
STEP = 10
SHARD_SIZES = (8, 2, 4)
INTERPRET = False

HIGH = lax.Precision.HIGHEST
NS_A = 3.4445
NS_B = -4.775
NS_C = 2.0315
CLIP_NORM = 0.01
LR_MUON = 0.5
MOMENT_DECAY = 0.5
BETA_ONE = 0.5
BETA_TWO = 0.5
ADAM_EPS = 1e-08
LN_EPS = 1e-06

BF = jnp.bfloat16
F32 = jnp.float32

SHARD = ("z", "yh", "x")
PLANE = ("x", "yh", "yl")
ROWS = ("z", "x")
YS = ("yh", "yl")
ALL = ("z", "yh", "x", "yl", "c")


def dot(lhs, rhs, lhs_dim, rhs_dim, precision=None):
    return lax.dot_general(
        lhs,
        rhs,
        (((lhs_dim,), (rhs_dim,)), ((), ())),
        precision=precision,
        preferred_element_type=F32,
    )


def rounded(v):
    return lax.reduce_precision(v.astype(F32), 8, 7)


def exchange(v, axes):
    return lax.all_to_all(v, axes, 0, 0)


def to_all(v, axes):
    return exchange(jnp.broadcast_to(v[None], (lax.axis_size(axes),) + v.shape), axes)


def swap(v, axis):
    return lax.ppermute(v, axis, [(0, 1), (1, 0)])


def added(one, two):
    return (one.astype(F32) + two.astype(F32)).astype(BF)


def in_order(index, mine, other, axis):
    return jnp.where(
        index == 0,
        jnp.concatenate([mine, other], axis=axis),
        jnp.concatenate([other, mine], axis=axis),
    )


def join_y(low, high):
    cut = 3 * low.shape[-1] // 4
    return jnp.concatenate(
        [low[..., :cut], high[..., :cut], low[..., cut:], high[..., cut:]], axis=-1
    )


def split_y(v, side):
    width = v.shape[-1] // 8
    return jnp.concatenate(
        [
            v[..., 3 * side * width : 3 * (side + 1) * width],
            v[..., (6 + side) * width : (7 + side) * width],
        ],
        axis=-1,
    )


def arranged(v, back=False):
    n_yh, n_x = lax.axis_size("yh"), lax.axis_size("x")
    first, second = (n_x, n_yh) if back else (n_yh, n_x)
    shape = v.shape
    v = v.reshape(shape[:-1] + (-1, first, second, RB))
    return jnp.swapaxes(v, -2, -3).reshape(shape)


def grid_table():
    quarter = D // 4
    feature = arranged(jnp.arange(D))
    part = feature // quarter
    rates = jnp.exp(-math.log(10000.0) * (feature % quarter).astype(F32) / quarter)
    phases = jnp.arange(GRID).astype(F32)[:, None] * rates[None, :]
    waves = jnp.where(part % 2 == 0, jnp.sin(phases), jnp.cos(phases))
    return jnp.where(part < 2, waves[None], waves[:, None]).reshape(SEQ, D)


def layer_norm(values):
    center = jnp.mean(values, axis=-1, keepdims=True)
    shifted = values - center
    inv_std = lax.rsqrt(jnp.mean(shifted * shifted, axis=-1, keepdims=True) + LN_EPS)
    return (shifted * inv_std, inv_std)


def norm_back(grad_norm, normed, inv_std):
    return inv_std * (
        grad_norm
        - jnp.mean(grad_norm, axis=-1, keepdims=True)
        - normed * jnp.mean(grad_norm * normed, axis=-1, keepdims=True)
    )


def gelu_tanh(values):
    return jax.nn.gelu(values, approximate=True)


def newton_kernel(gram_ref, norm_ref, out_ref):
    size = gram_ref.shape[-1]
    rows = lax.broadcasted_iota(jnp.int32, (size, size), 0)
    cols = lax.broadcasted_iota(jnp.int32, (size, size), 1)
    eye = (rows == cols).astype(F32)
    groups = gram_ref.shape[0]
    inv = [1.0 / norm_ref[g] for g in range(groups)]
    quad = [gram_ref[g] * (inv[g] * inv[g]) for g in range(groups)]
    total = [None] * groups

    def mul(a, b):
        return jnp.dot(a, b, precision=HIGH, preferred_element_type=F32)

    for turn in range(NS_STEPS):
        poly = [NS_A * eye + NS_B * q + NS_C * mul(q, q) for q in quad]
        total = [p if turn == 0 else mul(p, t) for p, t in zip(poly, total)]
        if turn < NS_STEPS - 1:
            half = [mul(p, q) for p, q in zip(poly, quad)]
            quad = [mul(h, p) for h, p in zip(half, poly)]
    for g in range(groups):
        out_ref[g] = total[g] * inv[g]


def newton_maps(grams):
    size = 8 * RB
    groups = grams.shape[0] // 8
    norms = jnp.sqrt(jnp.einsum("bii->b", grams)) + 1e-07
    place = jnp.arange(size) // RB
    same = (place[:, None] == place[None, :])[None]
    tiled = jnp.tile(grams.reshape(groups, size, RB), (1, 1, 8))
    blocks = jnp.where(same, tiled, 0.0)
    norm_rows = jnp.broadcast_to(
        jnp.repeat(norms, RB).reshape(groups, size, 1), (groups, size, size)
    )
    return pl.pallas_call(
        newton_kernel,
        out_shape=jax.ShapeDtypeStruct((groups, size, size), F32),
        interpret=INTERPRET,
    )(blocks, norm_rows)


def adam(weight, first_old, second_old, grad_in, step_rate):
    first_new = BETA_ONE * first_old + (1.0 - BETA_ONE) * grad_in
    second_new = BETA_TWO * second_old + (1.0 - BETA_TWO) * grad_in * grad_in
    fix_one = 1.0 - BETA_ONE**STEP
    fix_two = 1.0 - BETA_TWO**STEP
    new_weight = weight - step_rate * (first_new / fix_one) / (
        jnp.sqrt(second_new / fix_two) + ADAM_EPS
    )
    return (new_weight, first_new, second_new)


def across_rows(lhs, rhs):
    return dot(lhs, rhs, 1, 1)


def head_probs(q, k, side):
    lane = lax.broadcasted_iota(jnp.int32, (1, 2 * HDIM), 1)
    mask = (lane // HDIM == side).astype(F32)
    scores = across_rows((q.astype(F32) * mask).astype(BF), k) * (1.0 / math.sqrt(HDIM))
    grown = jnp.exp(scores - jnp.max(scores, axis=-1, keepdims=True))
    return grown / jnp.sum(grown, axis=-1, keepdims=True), mask


def attend_kernel(q_ref, k_ref, v_ref, out_ref):
    q, k, v = q_ref[...], k_ref[...], v_ref[...]
    out = 0.0
    for side in range(2):
        probs, mask = head_probs(q, k, side)
        out = out + mask * dot(probs.astype(BF), v, 1, 0)
    out_ref[...] = out.astype(BF)


def attend_back_kernel(*refs):
    block = pl.program_id(0)
    per = pl.num_programs(0) // 2
    for half in range(2):
        q, k, v, d_att = (r[...] for r in refs[4 * half : 4 * half + 4])
        d_q, d_k, d_v = 0.0, 0.0, 0.0
        for side in range(2):
            probs, mask = head_probs(q, k, side)
            d_probs = across_rows((d_att.astype(F32) * mask).astype(BF), v)
            d_v = d_v + mask * dot(probs.astype(BF), d_att, 0, 0)
            row_dot = jnp.sum(d_probs * probs, axis=-1, keepdims=True)
            d_raw = (probs * (d_probs - row_dot) * (1.0 / math.sqrt(HDIM))).astype(BF)
            d_q = d_q + mask * dot(d_raw, k, 1, 0)
            d_k = d_k + mask * dot(d_raw, q, 0, 0)
        for at, value in enumerate((d_q, d_k, d_v)):
            where = pl.multiple_of(qkv_block(block, at, per) * 2 * HDIM, 2 * HDIM)
            refs[8 + half][:, pl.ds(where, 2 * HDIM)] = value.astype(BF)


def qkv_block(j, at, per):
    return (j // per) * 3 * per + at * per + j % per


def columns(at=None, per=1):
    if at is None:
        return pl.BlockSpec((SEQ, 2 * HDIM), lambda j: (0, j))
    return pl.BlockSpec((SEQ, 2 * HDIM), lambda j: (0, qkv_block(j, at, per)))


def attend(qkv):
    width = qkv.shape[1] // 3
    groups = width // (2 * HDIM)
    return pl.pallas_call(
        attend_kernel,
        grid=(groups,),
        in_specs=[columns(at, groups // 2) for at in range(3)],
        out_specs=columns(),
        out_shape=jax.ShapeDtypeStruct((SEQ, width), BF),
        cost_estimate=pl.CostEstimate(
            flops=8 * SEQ * SEQ * width, bytes_accessed=8 * SEQ * width, transcendentals=4 * SEQ * SEQ
        ),
        interpret=INTERPRET,
    )(qkv, qkv, qkv)


def attend_back(qkv, d_att):
    width = qkv[0].shape[1] // 3
    groups = width // (2 * HDIM)
    whole = pl.BlockSpec((SEQ, 3 * width), lambda j: (0, 0))
    return pl.pallas_call(
        attend_back_kernel,
        grid=(groups,),
        in_specs=([columns(at, groups // 2) for at in range(3)] + [columns()]) * 2,
        out_specs=[whole] * 2,
        out_shape=[jax.ShapeDtypeStruct((SEQ, 3 * width), BF)] * 2,
        cost_estimate=pl.CostEstimate(
            flops=40 * SEQ * SEQ * width, bytes_accessed=28 * SEQ * width, transcendentals=8 * SEQ * SEQ
        ),
        interpret=INTERPRET,
    )(*(qkv[0],) * 3, d_att[0], *(qkv[1],) * 3, d_att[1])


def on_device(
    noisy_patches,
    true_noise,
    timesteps,
    labels,
    attn_w,
    attn_mom,
    mlp_w,
    mlp_mom,
    mod_w,
    mod_mom,
    temb_w,
    temb_mom,
    label_table,
    table_first,
    table_second,
    io_w,
    io_first,
    io_second,
    vec_w,
    vec_first,
    vec_second,
    head_b,
    headb_first,
    headb_second,
):
    n_shard = lax.axis_size(SHARD)
    n_all = lax.axis_size(ALL)
    count_all = n_all * SEQ * PATCH
    yl, core = lax.axis_index("yl"), lax.axis_index("c")
    sub = 2 * yl + core
    shard = lax.axis_index(SHARD)
    half = D // 2
    quarter = D // 4
    wide = 4 * half

    n_x = lax.axis_size("x")
    attn_low = lax.dynamic_slice_in_dim(attn_w, core * quarter, quarter, axis=2).astype(BF)
    attn_own = attn_low.transpose(1, 0, 2).reshape(RB, 4 * quarter)
    mlp_low = (
        lax.dynamic_slice_in_dim(mlp_w.reshape(2, 4, RB, half), 2 * yl, 2, axis=1)
        .astype(BF)
        .transpose(0, 2, 1, 3)
        .reshape(2, RB, D)
    )
    label_own = lax.dynamic_index_in_dim(labels, sub, keepdims=False)
    time_own = lax.dynamic_index_in_dim(timesteps, sub, keepdims=False)
    vec_cols = vec_w.shape[1]
    lanes_io = vec_w.shape[0]
    lanes_int = lanes_io + 2 * PATCH
    lanes_mod = 64
    lanes_all = 128
    ints = jnp.stack([label_own // 32, label_own % 32, time_own // 32, time_own % 32])
    common = jnp.concatenate(
        [
            vec_w.T.astype(BF),
            io_w.reshape(2 * PATCH, vec_cols).T.astype(BF),
            jnp.broadcast_to(ints.astype(BF)[None], (vec_cols, 4)),
            jnp.zeros((vec_cols, lanes_mod - lanes_int - 4), BF),
        ],
        axis=1,
    )
    mod_own = mod_w.astype(BF)
    mod_cols = (
        lax.dynamic_slice_in_dim(mod_own, sub * 4, 4, axis=1)
        .reshape(4, 2, 4, n_shard, RB)
        .transpose(3, 0, 2, 1, 4)
        .reshape(n_all, 4, 2 * RB)
    )
    sent = jnp.concatenate(
        [
            jnp.broadcast_to(common[None], (n_all,) + common.shape),
            mod_cols,
            jnp.zeros((n_all, 4, lanes_all - lanes_mod - 2 * RB), BF),
        ],
        axis=2,
    )
    y_rows = to_all(jnp.concatenate([attn_own, mlp_low[0], mlp_low[1]], axis=1), YS)
    y_rows, sent = lax.optimization_barrier((y_rows.reshape(2, 2, RB, 3 * D), sent))
    all_mine = lax.all_gather(
        jnp.concatenate([y_rows[:, 0], y_rows[:, 1]], axis=-1).reshape(2 * RB, 6 * D),
        ROWS,
        axis=0,
        tiled=True,
    )
    got = exchange(sent, ALL)
    marks = got[:, 0, lanes_int : lanes_int + 4].astype(F32)
    labels_all = (marks[:, 0] * 32.0 + marks[:, 1]).astype(jnp.int32)
    times_all = marks[:, 2] * 32.0 + marks[:, 3]
    by_feature = got.reshape(D, lanes_all)
    by_row = by_feature[:, :lanes_int].astype(F32).T
    vec_f = by_row[:lanes_io]
    vec_x = arranged(jnp.stack([vec_f[0], vec_f[13], vec_f[18]]))
    io_low = arranged(by_row[lanes_io:lanes_int].astype(BF))
    mod_col = by_feature[:, lanes_mod : lanes_mod + 2 * RB]
    own_features = lax.dynamic_slice_in_dim(by_feature, shard * RB, RB, axis=0)[
        :, :lanes_io
    ].astype(F32)
    own_mod_bias = lax.dynamic_slice_in_dim(own_features, 3 + 2 * sub, 2, axis=1)

    rates = jnp.exp(-math.log(10000.0) * jnp.arange(FREQ // 2, dtype=F32) / (FREQ // 2))
    phases = rates[:, None] * times_all[None, :]
    freq_t = jnp.concatenate([jnp.cos(phases), jnp.sin(phases)], axis=0).astype(BF)
    temb_low = temb_w.astype(BF)
    pre_t = dot(temb_low[:, :FREQ], freq_t, 1, 0) + own_features[:, 1:2]
    hid_t = jax.nn.silu(pre_t).astype(BF)
    temb_cols = lax.dynamic_slice_in_dim(
        temb_low[:, FREQ:].reshape(RB, n_shard, 4, vec_cols), sub, 1, axis=2
    ).reshape(RB, n_shard * vec_cols)
    cond_parts = dot(temb_cols, hid_t, 0, 0)
    cond_parts = exchange(
        cond_parts.reshape(n_shard, vec_cols, n_all), SHARD
    )
    onehot = (labels_all[:, None] == jnp.arange(NCLS)[None, :]).astype(BF)
    label_rows = dot(label_table.astype(BF), onehot, 0, 1)
    cond_t = jnp.sum(cond_parts, axis=0) + label_rows + rounded(vec_w[2])[:, None]
    act_own = jax.nn.silu(cond_t).astype(BF)
    act_t = to_all(act_own, ALL)
    patch_vals = lax.dynamic_index_in_dim(noisy_patches, sub, keepdims=False).reshape(SEQ, PATCH)
    x_in = dot(patch_vals, io_low[:PATCH], 1, 0) + vec_x[0] + grid_table()
    norm_one, inv_one = layer_norm(x_in)
    act_t, norm_one = lax.optimization_barrier((act_t, norm_one))
    act_t = act_t.reshape(D, n_all)
    mods_sent = dot(act_t, mod_col, 0, 0) + own_mod_bias.T.reshape(1, 2 * RB)
    mods = exchange(mods_sent[:, None], ALL).reshape(n_shard, 8, RB)
    mods = arranged(mods.transpose(1, 0, 2).reshape(8, 1, D))

    all_mine, mods = lax.optimization_barrier((all_mine, mods))
    attn_mine = join_y(all_mine[:, :D], all_mine[:, 3 * D : 4 * D])
    target = lax.dynamic_index_in_dim(true_noise, sub, keepdims=False).reshape(SEQ, PATCH)
    head_low = rounded(head_b)
    h_one = (norm_one * (1.0 + mods[1]) + mods[0]).astype(BF)
    own_half = (core, 1 - core)

    def attn_bias(row, which):
        rows = vec_f[row].reshape(2, 2, quarter)
        return lax.dynamic_index_in_dim(rows, which, axis=1, keepdims=False)


    def attention(weight, which):
        bias = jnp.stack(
            [attn_bias(11, which), jnp.zeros((2, quarter), F32), attn_bias(12, which)], axis=1
        )
        qkv = (dot(h_one, weight[:, : 3 * half], 1, 0) + bias.reshape(3 * half)).astype(BF)
        return qkv, attend(qkv)

    attn_other = swap(attn_mine, "c")
    qkv_mine, att_mine = attention(attn_mine, core)
    all_mine, attn_other, att_mine = lax.optimization_barrier((all_mine, attn_other, att_mine))
    qkv_other, att_other = attention(attn_other, 1 - core)
    attn_halves = (attn_mine, attn_other)
    qkv, attended = (qkv_mine, qkv_other), (att_mine, att_other)
    mlp_mine = jnp.concatenate(
        [all_mine[:, at : at + D] for at in (D, 4 * D, 2 * D, 5 * D)], axis=1
    )
    mlp_halves = (mlp_mine, swap(mlp_mine, "c"))
    first_halves = [m[:, :wide] for m in mlp_halves]
    second_halves = [m[:, wide:] for m in mlp_halves]
    attn_out = vec_x[1]
    for weight, att in zip(attn_halves, attended):
        attn_out = attn_out + dot(att, weight[:, 3 * half :], 1, 1)
    x_one = x_in + mods[2] * attn_out
    norm_two, inv_two = layer_norm(x_one)
    h_two = (norm_two * (1.0 + mods[4]) + mods[3]).astype(BF)
    pre_mlp = []
    act_mlp = []
    mlp_out = vec_x[2]
    for first, second, which in zip(first_halves, second_halves, own_half):
        bias = lax.dynamic_slice_in_dim(vec_f[14:18], which * half, half, axis=1).reshape(wide)
        pre = dot(h_two, first, 1, 0) + bias
        act = gelu_tanh(pre).astype(BF)
        pre_mlp.append(pre)
        act_mlp.append(act)
        mlp_out = mlp_out + dot(act, second, 1, 1)
    x_two = x_one + mods[5] * mlp_out
    norm_fin, inv_fin = layer_norm(x_two)
    y_low = (norm_fin * (1.0 + mods[7]) + mods[6]).astype(BF)
    pred_error = dot(y_low, io_low[PATCH:], 1, 1) + head_low - target.astype(F32)
    loss_own = jnp.sum(pred_error * pred_error)

    d_pred = pred_error * (2.0 / count_all)
    d_pred_low = d_pred.astype(BF)
    grad_head = dot(d_pred_low, y_low, 0, 0)
    grad_hb = jnp.sum(d_pred, axis=0)
    d_y = dot(d_pred_low, io_low[PATCH:], 1, 0)
    d_shift_fin = jnp.sum(d_y, axis=0)
    d_scale_fin = jnp.sum(d_y * norm_fin, axis=0)
    d_two = norm_back(d_y * (1.0 + mods[7]), norm_fin, inv_fin)
    d_gate_two = jnp.sum(d_two * mlp_out, axis=0)
    d_mlp = mods[5] * d_two
    d_mlp_low = d_mlp.astype(BF)
    grad_bfc = jnp.sum(d_mlp, axis=0)
    second_swap = swap(dot(d_mlp_low, act_mlp[1], 0, 0).astype(BF), "c")
    d_pre_low = []
    hid_bias = []
    for pre, second in zip(pre_mlp, second_halves):
        d_act = dot(d_mlp_low, second, 1, 0)
        d_pre = jax.vjp(gelu_tanh, pre)[1](d_act)[0]
        hid_bias.append(jnp.sum(d_pre, axis=0).reshape(4, half))
        d_pre_low.append(d_pre.astype(BF))
    second_swap, *d_pre_low = lax.optimization_barrier((second_swap, *d_pre_low))
    second_sum = (dot(d_mlp_low, act_mlp[0], 0, 0) + second_swap.astype(F32)).astype(BF)
    second_parts = second_sum.reshape(-1, 2 * n_x, RB, wide)
    second_sent = jnp.stack(
        [second_parts[..., at : at + D].transpose(1, 0, 2, 3) for at in (0, D)], axis=1
    ).reshape(4 * n_x, -1, D)
    second_sent, *d_pre_low = lax.optimization_barrier((second_sent, *d_pre_low))
    second_got = exchange(second_sent, PLANE)
    first_swap = swap(dot(h_two, d_pre_low[1], 0, 0).astype(BF), "c")
    d_h_two = dot(d_pre_low[0], first_halves[0], 1, 1) + dot(d_pre_low[1], first_halves[1], 1, 1)
    first_swap, d_h_two = lax.optimization_barrier((first_swap, d_h_two))
    first_sum = (dot(h_two, d_pre_low[0], 0, 0) + first_swap.astype(F32)).astype(BF)
    grad_bhid = in_order(core, hid_bias[0], hid_bias[1], 1)
    d_shift_two = jnp.sum(d_h_two, axis=0)
    d_scale_two = jnp.sum(d_h_two * norm_two, axis=0)
    d_one = d_two + norm_back(d_h_two * (1.0 + mods[4]), norm_two, inv_two)
    d_gate_one = jnp.sum(d_one * attn_out, axis=0)
    d_attn = mods[2] * d_one
    d_attn_low, first_sum = lax.optimization_barrier((d_attn.astype(BF), first_sum))
    first_z = lax.psum_scatter(first_sum, "z", scatter_dimension=0, tiled=True)
    grad_bout = jnp.sum(d_attn, axis=0)
    d_att = [dot(d_attn_low, weight[:, 3 * half :], 1, 0).astype(BF) for weight in attn_halves]
    d_proj = attend_back(qkv, d_att)
    d_h_one = sum(
        dot(d, weight[:, : 3 * half], 1, 1) for d, weight in zip(d_proj, attn_halves)
    )
    qv_bias = [
        jnp.sum(d.astype(F32), axis=0).reshape(2, 3, quarter)[:, ::2].transpose(1, 0, 2)[:, :, None]
        for d in d_proj
    ]
    grad_bqv = in_order(core, qv_bias[0], qv_bias[1], 2).reshape(2, D)
    d_shift_one = jnp.sum(d_h_one, axis=0)
    d_scale_one = jnp.sum(d_h_one * norm_one, axis=0)
    d_in = d_one + norm_back(d_h_one * (1.0 + mods[1]), norm_one, inv_one)
    grad_patch = dot(patch_vals, d_in.astype(BF), 0, 0)
    grad_bpatch = jnp.sum(d_in, axis=0)
    d_mods = jnp.stack(
        [
            d_shift_one,
            d_scale_one,
            d_gate_one,
            d_shift_two,
            d_scale_two,
            d_gate_two,
            d_shift_fin,
            d_scale_fin,
        ]
    )
    dmods_sent = arranged(d_mods, True)

    lanes = 128
    small = jnp.concatenate(
        [
            grad_bpatch[None],
            d_mods,
            arranged(grad_bqv),
            grad_bout[None],
            arranged(grad_bhid),
            grad_bfc[None],
            grad_patch,
            grad_head,
        ],
        axis=0,
    )
    n_small = small.shape[0]
    small = jnp.pad(small, ((0, lanes - n_small), (0, 0))).T.astype(BF)
    tiles = 2 * D // lanes
    dmod_sent = jnp.broadcast_to(
        dmods_sent.astype(BF).reshape(1, 4, tiles, lanes), (n_shard, 4, tiles, lanes)
    ).reshape(n_all, tiles, lanes)
    dmod_sent, second_got = lax.optimization_barrier((dmod_sent, second_got))
    dmod_all = exchange(dmod_sent, ALL)
    small, *held = lax.optimization_barrier((small, *d_proj))
    held[0], second_got = lax.optimization_barrier((held[0], second_got))
    grads = [
        jnp.concatenate(
            [dot(h_one, d, 0, 0).astype(BF), dot(d_attn_low, att, 0, 0).astype(BF), small], axis=1
        )
        for d, att in zip(held, attended)
    ]
    second_z = jnp.sum(second_got.astype(F32), axis=0).astype(BF).reshape(-1, RB, D)
    second_z, dmod_all = lax.optimization_barrier((second_z, dmod_all))
    second_back = exchange(second_z, "z")
    attn_sum, first_z = lax.optimization_barrier((chip_sum(grads), first_z))
    attn_z = lax.psum_scatter(attn_sum, "z", scatter_dimension=0, tiled=True)

    mod_sub = lax.dynamic_slice_in_dim(mod_own, 2 * sub, 2, axis=0)
    act_rows = lax.dynamic_slice_in_dim(act_t, shard * RB, RB, axis=0)
    dmod_all = dmod_all.reshape(n_all, 2 * D)
    grad_mod = dot(act_rows, dmod_all, 1, 0).reshape(RB, 2, D).transpose(1, 0, 2)
    d_act = dot(mod_sub.transpose(1, 0, 2).reshape(RB, 2 * D), dmod_all, 1, 1)
    d_act = d_act + swap(d_act, "c")
    d_act = d_act + swap(d_act, "yl")
    d_act = lax.dynamic_slice_in_dim(d_act, sub * vec_cols, vec_cols, axis=0)
    d_cond = jax.vjp(jax.nn.silu, cond_t)[1](d_act)[0]
    grad_table = dot(onehot.astype(F32), d_cond, 0, 1, HIGH)
    grad_bt_two = jnp.sum(d_cond, axis=1)
    d_cond_low = d_cond.astype(BF)
    d_cond_t = to_all(d_cond_low, ALL).reshape(D, n_all)
    d_hidden = dot(temb_low[:, FREQ:], d_cond_t, 1, 0)
    d_pre_time = jax.vjp(jax.nn.silu, pre_t)[1](d_hidden)[0]
    grad_bt_one = lax.dynamic_slice_in_dim(
        jnp.sum(d_pre_time, axis=1), sub * vec_cols, vec_cols, axis=0
    )
    grad_temb = jnp.concatenate(
        [dot(d_pre_time.astype(BF), freq_t, 1, 1), dot(hid_t, d_cond_t, 1, 1)], axis=1
    )

    mod_c = in_order(core, grad_mod, swap(grad_mod, "c"), 0)
    mod_s = in_order(yl, mod_c, swap(mod_c, "yl"), 0)
    rows = (2 * n_x, RB, -1)
    attn_z, first_z = attn_z.reshape(rows), first_z.reshape(rows)
    plane_sent = jnp.stack(
        [
            jnp.concatenate(
                [
                    split_y(attn_z[..., :wide], side),
                    first_z[..., side * D : (side + 1) * D],
                    attn_z[..., wide:],
                ],
                axis=-1,
            )
            for side in range(2)
        ],
        axis=1,
    ).reshape(4 * n_x, RB, 2 * D + lanes)
    plane_sent, mod_s = lax.optimization_barrier((plane_sent, mod_s))
    plane_own = jnp.sum(exchange(plane_sent, PLANE).astype(F32), axis=0)
    attn_q = plane_own[:, :D]
    mlp_q = jnp.stack([plane_own[:, D : 2 * D], jnp.sum(second_back.astype(F32), axis=0)])
    small_own = lax.dynamic_slice_in_dim(plane_own[:, 2 * D :], sub * vec_cols, vec_cols, axis=0).T
    vec_s = jnp.concatenate(
        [small_own[:1], grad_bt_one[None], grad_bt_two[None], small_own[1:17]], axis=0
    )
    io_s = small_own[17:n_small].reshape(2, PATCH, vec_cols)

    grads_square = jnp.sum(attn_q * attn_q) + jnp.sum(mlp_q * mlp_q)
    attn_q = attn_q.reshape(RB, 4, quarter).transpose(1, 0, 2)
    attn_s = in_order(core, attn_q, swap(attn_q, "c"), 2)
    mlp_s = (
        in_order(yl, mlp_q, swap(mlp_q, "yl"), 2)
        .reshape(2, RB, 4, half)
        .transpose(0, 2, 1, 3)
        .reshape(8, RB, half)
    )

    local_square = (
        grads_square
        + 0.25 * (jnp.sum(mod_s * mod_s) + jnp.sum(grad_temb * grad_temb))
        + jnp.sum(grad_table * grad_table)
        + jnp.sum(io_s * io_s)
        + jnp.sum(vec_s * vec_s)
    )
    sums = jnp.concatenate([local_square[None], loss_own[None], grad_hb])
    sums = jnp.pad(sums, (0, 128 - sums.shape[0]))
    sums = jnp.sum(to_all(sums[None], ALL), axis=0)[0]
    loss = sums[1] / count_all
    head_all = sums[2 : 2 + PATCH]
    grad_norm = jnp.sqrt(sums[0] + jnp.sum(head_all * head_all))
    factor = jnp.minimum(1.0, CLIP_NORM / (grad_norm + 1e-06))

    attn_moment = MOMENT_DECAY * attn_mom + factor * attn_s
    mlp_moment = MOMENT_DECAY * mlp_mom + factor * mlp_s
    mod_moment = MOMENT_DECAY * mod_mom + factor * mod_s
    temb_moment = MOMENT_DECAY * temb_mom + factor * grad_temb
    gram_attn = jnp.einsum("bij,bkj->bik", attn_moment, attn_moment, precision=HIGH)
    gram_mlp = jnp.einsum("bij,bkj->bik", mlp_moment, mlp_moment, precision=HIGH)
    gram_mod = jnp.einsum("bij,bkj->bik", mod_moment, mod_moment, precision=HIGH)
    temb_left, temb_right = temb_moment[:, :FREQ], temb_moment[:, FREQ:]
    gram_left = dot(temb_left, temb_left, 1, 1, HIGH)[None]
    gram_right = dot(temb_right, temb_right, 1, 1, HIGH)[None]
    gram_attn = gram_attn + swap(gram_attn, "yl")
    gram_mlp = gram_mlp + swap(gram_mlp, "c")
    maps = newton_maps(
        jnp.concatenate(
            [gram_attn, gram_left, gram_right, jnp.zeros((2, RB, RB), F32), gram_mlp, gram_mod]
        )
    )
    n_attn = 4 * RB
    attn_ortho = dot(
        maps[0, :n_attn, :n_attn], attn_moment.reshape(n_attn, half), 1, 0, HIGH
    ).reshape(attn_moment.shape)
    left_ortho = dot(
        maps[0, n_attn : n_attn + RB, n_attn : n_attn + RB], temb_left, 1, 0, HIGH
    )
    right_ortho = dot(
        maps[0, n_attn + RB : n_attn + 2 * RB, n_attn + RB : n_attn + 2 * RB],
        temb_right,
        1,
        0,
        HIGH,
    )
    mlp_ortho = dot(maps[1], mlp_moment.reshape(8 * RB, half), 1, 0, HIGH).reshape(
        mlp_moment.shape
    )
    mod_ortho = dot(maps[2], mod_moment.reshape(8 * RB, D), 1, 0, HIGH).reshape(mod_moment.shape)
    attn_new = attn_w - LR_MUON * attn_ortho
    mlp_new = mlp_w - LR_MUON * mlp_ortho
    mod_new = mod_w - LR_MUON * mod_ortho
    temb_new = temb_w - LR_MUON * jnp.concatenate([left_ortho, right_ortho], axis=1)
    table_new, table_first_new, table_second_new = adam(
        label_table, table_first, table_second, factor * grad_table, 0.3
    )
    io_rates = jnp.array([0.1, 0.01], F32).reshape(2, 1, 1)
    io_new, io_first_new, io_second_new = adam(io_w, io_first, io_second, factor * io_s, io_rates)
    vec_new, vec_first_new, vec_second_new = adam(
        vec_w, vec_first, vec_second, factor * vec_s, 0.05
    )
    headb_new, headb_first_new, headb_second_new = adam(
        head_b, headb_first, headb_second, factor * head_all, 0.05
    )
    return (
        loss,
        grad_norm,
        attn_new,
        attn_moment,
        attn_new.astype(BF),
        mlp_new,
        mlp_moment,
        mlp_new.astype(BF),
        mod_new,
        mod_moment,
        mod_new.astype(BF),
        temb_new,
        temb_moment,
        table_new,
        table_first_new,
        table_second_new,
        table_new.astype(BF),
        io_new,
        io_first_new,
        io_second_new,
        vec_new,
        vec_first_new,
        vec_second_new,
        headb_new,
        headb_first_new,
        headb_second_new,
    )


def chip_sum(halves):
    mine, other = halves
    return (mine.astype(F32) + swap(other, "c").astype(F32)).astype(BF)


def solution(mesh):
    fine = Mesh(mesh.devices.reshape(SHARD_SIZES + (2, 2)), ALL)
    lat = P(SHARD, None)
    one = P(SHARD)
    attn = P(None, SHARD, "yl")
    mlp = P(None, SHARD, "c")
    mod = P(None, SHARD, None)
    temb = P(SHARD, None)
    flat = P(None, ALL)
    io = P(None, None, ALL)
    rep = P()
    return jax.shard_map(
        on_device,
        mesh=fine,
        in_specs=(lat, lat, one, one, attn, attn, mlp, mlp, mod, mod, temb, temb)
        + (flat,) * 3
        + (io,) * 3
        + (flat,) * 3
        + (rep,) * 3,
        out_specs=(rep, rep)
        + (attn,) * 3
        + (mlp,) * 3
        + (mod,) * 3
        + (temb,) * 2
        + (flat,) * 4
        + (io,) * 3
        + (flat,) * 3
        + (rep,) * 3,
        check_vma=False,
    )
```

```python
import functools
import math

import jax
import jax.numpy as jnp
from jax import lax
from jax.experimental import pallas as pl
from jax.experimental.pallas import tpu as pltpu
from jax.sharding import Mesh
from jax.sharding import PartitionSpec as P

D = 1024
HDIM = 64
FREQ = 256
NCLS = 1000
PATCH = 16
GRID = 16
SEQ = 256
RB = 16
NS_STEPS = 5
STEP = 10
SHARD_SIZES = (8, 2, 4)
INTERPRET = False

HIGH = lax.Precision.HIGHEST
NS_A = 3.4445
NS_B = -4.775
NS_C = 2.0315
CLIP_NORM = 0.01
LR_MUON = 0.5
MOMENT_DECAY = 0.5
BETA_ONE = 0.5
BETA_TWO = 0.5
ADAM_EPS = 1e-08
LN_EPS = 1e-06

BF = jnp.bfloat16
F32 = jnp.float32

SHARD = ("z", "yh", "x")
PLANE = ("x", "yh", "yl")
ROWS = ("z", "x")
YS = ("yh", "yl")
ALL = ("z", "yh", "x", "yl", "c")


def dot(lhs, rhs, lhs_dim, rhs_dim, precision=None):
    return lax.dot_general(
        lhs,
        rhs,
        (((lhs_dim,), (rhs_dim,)), ((), ())),
        precision=precision,
        preferred_element_type=F32,
    )


def rounded(v):
    return lax.reduce_precision(v.astype(F32), 8, 7)


def exchange(v, axes):
    return lax.all_to_all(v, axes, 0, 0)


def to_all(v, axes):
    return exchange(jnp.broadcast_to(v[None], (lax.axis_size(axes),) + v.shape), axes)


def swap(v, axis):
    return lax.ppermute(v, axis, [(0, 1), (1, 0)])


def added(one, two):
    return (one.astype(F32) + two.astype(F32)).astype(BF)


def in_order(index, mine, other, axis):
    return jnp.where(
        index == 0,
        jnp.concatenate([mine, other], axis=axis),
        jnp.concatenate([other, mine], axis=axis),
    )


def join_y(low, high):
    cut = 3 * low.shape[-1] // 4
    return jnp.concatenate(
        [low[..., :cut], high[..., :cut], low[..., cut:], high[..., cut:]], axis=-1
    )


def split_y(v, side):
    width = v.shape[-1] // 8
    return jnp.concatenate(
        [
            v[..., 3 * side * width : 3 * (side + 1) * width],
            v[..., (6 + side) * width : (7 + side) * width],
        ],
        axis=-1,
    )


def arranged(v, back=False):
    n_yh, n_x = lax.axis_size("yh"), lax.axis_size("x")
    first, second = (n_x, n_yh) if back else (n_yh, n_x)
    shape = v.shape
    v = v.reshape(shape[:-1] + (-1, first, second, RB))
    return jnp.swapaxes(v, -2, -3).reshape(shape)


def grid_table():
    quarter = D // 4
    feature = arranged(jnp.arange(D))
    part = feature // quarter
    rates = jnp.exp(-math.log(10000.0) * (feature % quarter).astype(F32) / quarter)
    phases = jnp.arange(GRID).astype(F32)[:, None] * rates[None, :]
    waves = jnp.where(part % 2 == 0, jnp.sin(phases), jnp.cos(phases))
    return jnp.where(part < 2, waves[None], waves[:, None]).reshape(SEQ, D)


def layer_norm(values):
    center = jnp.mean(values, axis=-1, keepdims=True)
    shifted = values - center
    inv_std = lax.rsqrt(jnp.mean(shifted * shifted, axis=-1, keepdims=True) + LN_EPS)
    return (shifted * inv_std, inv_std)


def norm_back(grad_norm, normed, inv_std):
    return inv_std * (
        grad_norm
        - jnp.mean(grad_norm, axis=-1, keepdims=True)
        - normed * jnp.mean(grad_norm * normed, axis=-1, keepdims=True)
    )


def gelu_tanh(values):
    return jax.nn.gelu(values, approximate=True)


def newton_kernel(gram_ref, norm_ref, out_ref):
    size = gram_ref.shape[-1]
    rows = lax.broadcasted_iota(jnp.int32, (size, size), 0)
    cols = lax.broadcasted_iota(jnp.int32, (size, size), 1)
    eye = (rows == cols).astype(F32)
    groups = gram_ref.shape[0]
    inv = [1.0 / norm_ref[g] for g in range(groups)]
    quad = [gram_ref[g] * (inv[g] * inv[g]) for g in range(groups)]
    total = [None] * groups

    def mul(a, b):
        return jnp.dot(a, b, precision=HIGH, preferred_element_type=F32)

    for turn in range(NS_STEPS):
        poly = [NS_A * eye + NS_B * q + NS_C * mul(q, q) for q in quad]
        total = [p if turn == 0 else mul(p, t) for p, t in zip(poly, total)]
        if turn < NS_STEPS - 1:
            half = [mul(p, q) for p, q in zip(poly, quad)]
            quad = [mul(h, p) for h, p in zip(half, poly)]
    for g in range(groups):
        out_ref[g] = total[g] * inv[g]


def newton_maps(grams):
    size = 8 * RB
    groups = grams.shape[0] // 8
    norms = jnp.sqrt(jnp.einsum("bii->b", grams)) + 1e-07
    place = jnp.arange(size) // RB
    same = (place[:, None] == place[None, :])[None]
    tiled = jnp.tile(grams.reshape(groups, size, RB), (1, 1, 8))
    blocks = jnp.where(same, tiled, 0.0)
    norm_rows = jnp.broadcast_to(
        jnp.repeat(norms, RB).reshape(groups, size, 1), (groups, size, size)
    )
    return pl.pallas_call(
        newton_kernel,
        out_shape=jax.ShapeDtypeStruct((groups, size, size), F32),
        interpret=INTERPRET,
    )(blocks, norm_rows)


def adam(weight, first_old, second_old, grad_in, step_rate):
    first_new = BETA_ONE * first_old + (1.0 - BETA_ONE) * grad_in
    second_new = BETA_TWO * second_old + (1.0 - BETA_TWO) * grad_in * grad_in
    fix_one = 1.0 - BETA_ONE**STEP
    fix_two = 1.0 - BETA_TWO**STEP
    new_weight = weight - step_rate * (first_new / fix_one) / (
        jnp.sqrt(second_new / fix_two) + ADAM_EPS
    )
    return (new_weight, first_new, second_new)


def across_rows(lhs, rhs):
    return dot(lhs, rhs, 1, 1)


def head_probs(q, k, side):
    lane = lax.broadcasted_iota(jnp.int32, (1, 2 * HDIM), 1)
    mask = (lane // HDIM == side).astype(F32)
    scores = across_rows((q.astype(F32) * mask).astype(BF), k) * (1.0 / math.sqrt(HDIM))
    grown = jnp.exp(scores - jnp.max(scores, axis=-1, keepdims=True))
    return grown / jnp.sum(grown, axis=-1, keepdims=True), mask


def attend_kernel(q_ref, k_ref, v_ref, out_ref):
    q, k, v = q_ref[...], k_ref[...], v_ref[...]
    out = 0.0
    for side in range(2):
        probs, mask = head_probs(q, k, side)
        out = out + mask * dot(probs.astype(BF), v, 1, 0)
    out_ref[...] = out.astype(BF)


def attend_back_kernel(*refs):
    block = pl.program_id(0)
    per = pl.num_programs(0) // 2
    for half in range(2):
        q, k, v, d_att = (r[...] for r in refs[4 * half : 4 * half + 4])
        d_q, d_k, d_v = 0.0, 0.0, 0.0
        for side in range(2):
            probs, mask = head_probs(q, k, side)
            d_probs = across_rows((d_att.astype(F32) * mask).astype(BF), v)
            d_v = d_v + mask * dot(probs.astype(BF), d_att, 0, 0)
            row_dot = jnp.sum(d_probs * probs, axis=-1, keepdims=True)
            d_raw = (probs * (d_probs - row_dot) * (1.0 / math.sqrt(HDIM))).astype(BF)
            d_q = d_q + mask * dot(d_raw, k, 1, 0)
            d_k = d_k + mask * dot(d_raw, q, 0, 0)
        for at, value in enumerate((d_q, d_k, d_v)):
            where = pl.multiple_of(qkv_block(block, at, per) * 2 * HDIM, 2 * HDIM)
            refs[8 + half][:, pl.ds(where, 2 * HDIM)] = value.astype(BF)


def qkv_block(j, at, per):
    return (j // per) * 3 * per + at * per + j % per


def columns(at=None, per=1):
    if at is None:
        return pl.BlockSpec((SEQ, 2 * HDIM), lambda j: (0, j))
    return pl.BlockSpec((SEQ, 2 * HDIM), lambda j: (0, qkv_block(j, at, per)))


def attend(qkv):
    width = qkv.shape[1] // 3
    groups = width // (2 * HDIM)
    return pl.pallas_call(
        attend_kernel,
        grid=(groups,),
        in_specs=[columns(at, groups // 2) for at in range(3)],
        out_specs=columns(),
        out_shape=jax.ShapeDtypeStruct((SEQ, width), BF),
        cost_estimate=pl.CostEstimate(
            flops=8 * SEQ * SEQ * width, bytes_accessed=8 * SEQ * width, transcendentals=4 * SEQ * SEQ
        ),
        interpret=INTERPRET,
    )(qkv, qkv, qkv)


def attend_back(qkv, d_att):
    width = qkv[0].shape[1] // 3
    groups = width // (2 * HDIM)
    whole = pl.BlockSpec((SEQ, 3 * width), lambda j: (0, 0))
    return pl.pallas_call(
        attend_back_kernel,
        grid=(groups,),
        in_specs=([columns(at, groups // 2) for at in range(3)] + [columns()]) * 2,
        out_specs=[whole] * 2,
        out_shape=[jax.ShapeDtypeStruct((SEQ, 3 * width), BF)] * 2,
        cost_estimate=pl.CostEstimate(
            flops=40 * SEQ * SEQ * width, bytes_accessed=28 * SEQ * width, transcendentals=8 * SEQ * SEQ
        ),
        interpret=INTERPRET,
    )(*(qkv[0],) * 3, d_att[0], *(qkv[1],) * 3, d_att[1])


def on_device(
    noisy_patches,
    true_noise,
    timesteps,
    labels,
    attn_w,
    attn_mom,
    mlp_w,
    mlp_mom,
    mod_w,
    mod_mom,
    temb_w,
    temb_mom,
    label_table,
    table_first,
    table_second,
    io_w,
    io_first,
    io_second,
    vec_w,
    vec_first,
    vec_second,
    head_b,
    headb_first,
    headb_second,
):
    n_shard = lax.axis_size(SHARD)
    n_all = lax.axis_size(ALL)
    count_all = n_all * SEQ * PATCH
    yl, core = lax.axis_index("yl"), lax.axis_index("c")
    sub = 2 * yl + core
    shard = lax.axis_index(SHARD)
    half = D // 2
    quarter = D // 4
    wide = 4 * half

    n_x = lax.axis_size("x")
    attn_low = lax.dynamic_slice_in_dim(attn_w, core * quarter, quarter, axis=2).astype(BF)
    attn_own = attn_low.transpose(1, 0, 2).reshape(RB, 4 * quarter)
    mlp_low = (
        lax.dynamic_slice_in_dim(mlp_w.reshape(2, 4, RB, half), 2 * yl, 2, axis=1)
        .astype(BF)
        .transpose(0, 2, 1, 3)
        .reshape(2, RB, D)
    )
    label_own = lax.dynamic_index_in_dim(labels, sub, keepdims=False)
    time_own = lax.dynamic_index_in_dim(timesteps, sub, keepdims=False)
    vec_cols = vec_w.shape[1]
    lanes_io = vec_w.shape[0]
    lanes_int = lanes_io + 2 * PATCH
    lanes_mod = 64
    lanes_all = 128
    ints = jnp.stack([label_own // 32, label_own % 32, time_own // 32, time_own % 32])
    common = jnp.concatenate(
        [
            vec_w.T.astype(BF),
            io_w.reshape(2 * PATCH, vec_cols).T.astype(BF),
            jnp.broadcast_to(ints.astype(BF)[None], (vec_cols, 4)),
            jnp.zeros((vec_cols, lanes_mod - lanes_int - 4), BF),
        ],
        axis=1,
    )
    mod_own = mod_w.astype(BF)
    mod_cols = (
        lax.dynamic_slice_in_dim(mod_own, sub * 4, 4, axis=1)
        .reshape(4, 2, 4, n_shard, RB)
        .transpose(3, 0, 2, 1, 4)
        .reshape(n_all, 4, 2 * RB)
    )
    sent = jnp.concatenate(
        [
            jnp.broadcast_to(common[None], (n_all,) + common.shape),
            mod_cols,
            jnp.zeros((n_all, 4, lanes_all - lanes_mod - 2 * RB), BF),
        ],
        axis=2,
    )
    y_rows = to_all(jnp.concatenate([attn_own, mlp_low[0], mlp_low[1]], axis=1), YS)
    y_rows = y_rows.reshape(2, 2, RB, 3 * D)
    all_mine = lax.all_gather(
        jnp.concatenate([y_rows[:, 0], y_rows[:, 1]], axis=-1).reshape(2 * RB, 6 * D),
        ROWS,
        axis=0,
        tiled=True,
    )
    got = exchange(sent, ALL)
    marks = got[:, 0, lanes_int : lanes_int + 4].astype(F32)
    labels_all = (marks[:, 0] * 32.0 + marks[:, 1]).astype(jnp.int32)
    times_all = marks[:, 2] * 32.0 + marks[:, 3]
    by_feature = got.reshape(D, lanes_all)
    by_row = by_feature[:, :lanes_int].astype(F32).T
    vec_f = by_row[:lanes_io]
    vec_x = arranged(jnp.stack([vec_f[0], vec_f[13], vec_f[18]]))
    io_low = arranged(by_row[lanes_io:lanes_int].astype(BF))
    mod_col = by_feature[:, lanes_mod : lanes_mod + 2 * RB]
    own_features = lax.dynamic_slice_in_dim(by_feature, shard * RB, RB, axis=0)[
        :, :lanes_io
    ].astype(F32)
    own_mod_bias = lax.dynamic_slice_in_dim(own_features, 3 + 2 * sub, 2, axis=1)

    rates = jnp.exp(-math.log(10000.0) * jnp.arange(FREQ // 2, dtype=F32) / (FREQ // 2))
    phases = rates[:, None] * times_all[None, :]
    freq_t = jnp.concatenate([jnp.cos(phases), jnp.sin(phases)], axis=0).astype(BF)
    temb_low = temb_w.astype(BF)
    pre_t = dot(temb_low[:, :FREQ], freq_t, 1, 0) + own_features[:, 1:2]
    hid_t = jax.nn.silu(pre_t).astype(BF)
    temb_cols = lax.dynamic_slice_in_dim(
        temb_low[:, FREQ:].reshape(RB, n_shard, 4, vec_cols), sub, 1, axis=2
    ).reshape(RB, n_shard * vec_cols)
    cond_parts = dot(temb_cols, hid_t, 0, 0)
    cond_parts = exchange(
        cond_parts.reshape(n_shard, vec_cols, n_all), SHARD
    )
    onehot = (labels_all[:, None] == jnp.arange(NCLS)[None, :]).astype(BF)
    label_rows = dot(label_table.astype(BF), onehot, 0, 1)
    cond_t = jnp.sum(cond_parts, axis=0) + label_rows + rounded(vec_w[2])[:, None]
    act_own = jax.nn.silu(cond_t).astype(BF)
    act_t = to_all(act_own, ALL)
    patch_vals = lax.dynamic_index_in_dim(noisy_patches, sub, keepdims=False).reshape(SEQ, PATCH)
    x_in = dot(patch_vals, io_low[:PATCH], 1, 0) + vec_x[0] + grid_table()
    norm_one, inv_one = layer_norm(x_in)
    act_t, norm_one = lax.optimization_barrier((act_t, norm_one))
    act_t = act_t.reshape(D, n_all)
    mods_sent = dot(act_t, mod_col, 0, 0) + own_mod_bias.T.reshape(1, 2 * RB)
    mods = exchange(mods_sent[:, None], ALL).reshape(n_shard, 8, RB)
    mods = arranged(mods.transpose(1, 0, 2).reshape(8, 1, D))

    all_mine, mods = lax.optimization_barrier((all_mine, mods))
    attn_mine = join_y(all_mine[:, :D], all_mine[:, 3 * D : 4 * D])
    target = lax.dynamic_index_in_dim(true_noise, sub, keepdims=False).reshape(SEQ, PATCH)
    head_low = rounded(head_b)
    h_one = (norm_one * (1.0 + mods[1]) + mods[0]).astype(BF)
    own_half = (core, 1 - core)

    def attn_bias(row, which):
        rows = vec_f[row].reshape(2, 2, quarter)
        return lax.dynamic_index_in_dim(rows, which, axis=1, keepdims=False)


    def attention(weight, which):
        bias = jnp.stack(
            [attn_bias(11, which), jnp.zeros((2, quarter), F32), attn_bias(12, which)], axis=1
        )
        qkv = (dot(h_one, weight[:, : 3 * half], 1, 0) + bias.reshape(3 * half)).astype(BF)
        return qkv, attend(qkv)

    attn_other = swap(attn_mine, "c")
    qkv_mine, att_mine = attention(attn_mine, core)
    all_mine, attn_other, att_mine = lax.optimization_barrier((all_mine, attn_other, att_mine))
    qkv_other, att_other = attention(attn_other, 1 - core)
    attn_halves = (attn_mine, attn_other)
    qkv, attended = (qkv_mine, qkv_other), (att_mine, att_other)
    mlp_mine = jnp.concatenate(
        [all_mine[:, at : at + D] for at in (D, 4 * D, 2 * D, 5 * D)], axis=1
    )
    mlp_halves = (mlp_mine, swap(mlp_mine, "c"))
    first_halves = [m[:, :wide] for m in mlp_halves]
    second_halves = [m[:, wide:] for m in mlp_halves]
    attn_out = vec_x[1]
    for weight, att in zip(attn_halves, attended):
        attn_out = attn_out + dot(att, weight[:, 3 * half :], 1, 1)
    x_one = x_in + mods[2] * attn_out
    norm_two, inv_two = layer_norm(x_one)
    h_two = (norm_two * (1.0 + mods[4]) + mods[3]).astype(BF)
    pre_mlp = []
    act_mlp = []
    mlp_out = vec_x[2]
    for first, second, which in zip(first_halves, second_halves, own_half):
        bias = lax.dynamic_slice_in_dim(vec_f[14:18], which * half, half, axis=1).reshape(wide)
        pre = dot(h_two, first, 1, 0) + bias
        act = gelu_tanh(pre).astype(BF)
        pre_mlp.append(pre)
        act_mlp.append(act)
        mlp_out = mlp_out + dot(act, second, 1, 1)
    x_two = x_one + mods[5] * mlp_out
    norm_fin, inv_fin = layer_norm(x_two)
    y_low = (norm_fin * (1.0 + mods[7]) + mods[6]).astype(BF)
    pred_error = dot(y_low, io_low[PATCH:], 1, 1) + head_low - target.astype(F32)
    loss_own = jnp.sum(pred_error * pred_error)

    d_pred = pred_error * (2.0 / count_all)
    d_pred_low = d_pred.astype(BF)
    grad_head = dot(d_pred_low, y_low, 0, 0)
    grad_hb = jnp.sum(d_pred, axis=0)
    d_y = dot(d_pred_low, io_low[PATCH:], 1, 0)
    d_shift_fin = jnp.sum(d_y, axis=0)
    d_scale_fin = jnp.sum(d_y * norm_fin, axis=0)
    d_two = norm_back(d_y * (1.0 + mods[7]), norm_fin, inv_fin)
    d_gate_two = jnp.sum(d_two * mlp_out, axis=0)
    d_mlp = mods[5] * d_two
    d_mlp_low = d_mlp.astype(BF)
    grad_bfc = jnp.sum(d_mlp, axis=0)
    second_swap = swap(dot(d_mlp_low, act_mlp[1], 0, 0).astype(BF), "c")
    d_pre_low = []
    hid_bias = []
    for pre, second in zip(pre_mlp, second_halves):
        d_act = dot(d_mlp_low, second, 1, 0)
        d_pre = jax.vjp(gelu_tanh, pre)[1](d_act)[0]
        hid_bias.append(jnp.sum(d_pre, axis=0).reshape(4, half))
        d_pre_low.append(d_pre.astype(BF))
    second_swap, *d_pre_low = lax.optimization_barrier((second_swap, *d_pre_low))
    second_sum = (dot(d_mlp_low, act_mlp[0], 0, 0) + second_swap.astype(F32)).astype(BF)
    second_parts = second_sum.reshape(-1, 2 * n_x, RB, wide)
    second_sent = jnp.stack(
        [second_parts[..., at : at + D].transpose(1, 0, 2, 3) for at in (0, D)], axis=1
    ).reshape(4 * n_x, -1, D)
    second_sent, *d_pre_low = lax.optimization_barrier((second_sent, *d_pre_low))
    second_got = exchange(second_sent, PLANE)
    first_swap = swap(dot(h_two, d_pre_low[1], 0, 0).astype(BF), "c")
    d_h_two = dot(d_pre_low[0], first_halves[0], 1, 1) + dot(d_pre_low[1], first_halves[1], 1, 1)
    first_swap, d_h_two = lax.optimization_barrier((first_swap, d_h_two))
    first_sum = (dot(h_two, d_pre_low[0], 0, 0) + first_swap.astype(F32)).astype(BF)
    grad_bhid = in_order(core, hid_bias[0], hid_bias[1], 1)
    d_shift_two = jnp.sum(d_h_two, axis=0)
    d_scale_two = jnp.sum(d_h_two * norm_two, axis=0)
    d_one = d_two + norm_back(d_h_two * (1.0 + mods[4]), norm_two, inv_two)
    d_gate_one = jnp.sum(d_one * attn_out, axis=0)
    d_attn = mods[2] * d_one
    d_attn_low, first_sum = lax.optimization_barrier((d_attn.astype(BF), first_sum))
    first_z = lax.psum_scatter(first_sum, "z", scatter_dimension=0, tiled=True)
    grad_bout = jnp.sum(d_attn, axis=0)
    d_att = [dot(d_attn_low, weight[:, 3 * half :], 1, 0).astype(BF) for weight in attn_halves]
    d_proj = attend_back(qkv, d_att)
    d_h_one = sum(
        dot(d, weight[:, : 3 * half], 1, 1) for d, weight in zip(d_proj, attn_halves)
    )
    qv_bias = [
        jnp.sum(d.astype(F32), axis=0).reshape(2, 3, quarter)[:, ::2].transpose(1, 0, 2)[:, :, None]
        for d in d_proj
    ]
    grad_bqv = in_order(core, qv_bias[0], qv_bias[1], 2).reshape(2, D)
    d_shift_one = jnp.sum(d_h_one, axis=0)
    d_scale_one = jnp.sum(d_h_one * norm_one, axis=0)
    d_in = d_one + norm_back(d_h_one * (1.0 + mods[1]), norm_one, inv_one)
    grad_patch = dot(patch_vals, d_in.astype(BF), 0, 0)
    grad_bpatch = jnp.sum(d_in, axis=0)
    d_mods = jnp.stack(
        [
            d_shift_one,
            d_scale_one,
            d_gate_one,
            d_shift_two,
            d_scale_two,
            d_gate_two,
            d_shift_fin,
            d_scale_fin,
        ]
    )
    dmods_sent = arranged(d_mods, True)

    lanes = 128
    small = jnp.concatenate(
        [
            grad_bpatch[None],
            d_mods,
            arranged(grad_bqv),
            grad_bout[None],
            arranged(grad_bhid),
            grad_bfc[None],
            grad_patch,
            grad_head,
        ],
        axis=0,
    )
    n_small = small.shape[0]
    small = jnp.pad(small, ((0, lanes - n_small), (0, 0))).T.astype(BF)
    tiles = 2 * D // lanes
    dmod_sent = jnp.broadcast_to(
        dmods_sent.astype(BF).reshape(1, 4, tiles, lanes), (n_shard, 4, tiles, lanes)
    ).reshape(n_all, tiles, lanes)
    dmod_sent, second_got = lax.optimization_barrier((dmod_sent, second_got))
    dmod_all = exchange(dmod_sent, ALL)
    small, *held = lax.optimization_barrier((small, *d_proj))
    held[0], second_got = lax.optimization_barrier((held[0], second_got))
    grads = [
        jnp.concatenate(
            [dot(h_one, d, 0, 0).astype(BF), dot(d_attn_low, att, 0, 0).astype(BF), small], axis=1
        )
        for d, att in zip(held, attended)
    ]
    second_z = jnp.sum(second_got.astype(F32), axis=0).astype(BF).reshape(-1, RB, D)
    second_z, dmod_all = lax.optimization_barrier((second_z, dmod_all))
    second_back = lax.psum_scatter(second_z.reshape(-1, D), "z", scatter_dimension=0, tiled=True)
    attn_sum, first_z = lax.optimization_barrier((chip_sum(grads), first_z))
    attn_z = lax.psum_scatter(attn_sum, "z", scatter_dimension=0, tiled=True)

    mod_sub = lax.dynamic_slice_in_dim(mod_own, 2 * sub, 2, axis=0)
    act_rows = lax.dynamic_slice_in_dim(act_t, shard * RB, RB, axis=0)
    dmod_all = dmod_all.reshape(n_all, 2 * D)
    grad_mod = dot(act_rows, dmod_all, 1, 0).reshape(RB, 2, D).transpose(1, 0, 2)
    d_act = dot(mod_sub.transpose(1, 0, 2).reshape(RB, 2 * D), dmod_all, 1, 1)
    d_act = d_act + swap(d_act, "c")
    d_act = d_act + swap(d_act, "yl")
    d_act = lax.dynamic_slice_in_dim(d_act, sub * vec_cols, vec_cols, axis=0)
    d_cond = jax.vjp(jax.nn.silu, cond_t)[1](d_act)[0]
    grad_table = dot(onehot.astype(F32), d_cond, 0, 1, HIGH)
    grad_bt_two = jnp.sum(d_cond, axis=1)
    d_cond_low = d_cond.astype(BF)
    d_cond_t = to_all(d_cond_low, ALL).reshape(D, n_all)
    d_hidden = dot(temb_low[:, FREQ:], d_cond_t, 1, 0)
    d_pre_time = jax.vjp(jax.nn.silu, pre_t)[1](d_hidden)[0]
    grad_bt_one = lax.dynamic_slice_in_dim(
        jnp.sum(d_pre_time, axis=1), sub * vec_cols, vec_cols, axis=0
    )
    grad_temb = jnp.concatenate(
        [dot(d_pre_time.astype(BF), freq_t, 1, 1), dot(hid_t, d_cond_t, 1, 1)], axis=1
    )

    mod_c = in_order(core, grad_mod, swap(grad_mod, "c"), 0)
    mod_s = in_order(yl, mod_c, swap(mod_c, "yl"), 0)
    rows = (2 * n_x, RB, -1)
    attn_z, first_z = attn_z.reshape(rows), first_z.reshape(rows)
    plane_sent = jnp.stack(
        [
            jnp.concatenate(
                [
                    split_y(attn_z[..., :wide], side),
                    first_z[..., side * D : (side + 1) * D],
                    attn_z[..., wide:],
                ],
                axis=-1,
            )
            for side in range(2)
        ],
        axis=1,
    ).reshape(4 * n_x, RB, 2 * D + lanes)
    plane_sent, mod_s = lax.optimization_barrier((plane_sent, mod_s))
    plane_own = jnp.sum(exchange(plane_sent, PLANE).astype(F32), axis=0)
    attn_q = plane_own[:, :D]
    mlp_q = jnp.stack([plane_own[:, D : 2 * D], second_back.astype(F32)])
    small_own = lax.dynamic_slice_in_dim(plane_own[:, 2 * D :], sub * vec_cols, vec_cols, axis=0).T
    vec_s = jnp.concatenate(
        [small_own[:1], grad_bt_one[None], grad_bt_two[None], small_own[1:17]], axis=0
    )
    io_s = small_own[17:n_small].reshape(2, PATCH, vec_cols)

    grads_square = jnp.sum(attn_q * attn_q) + jnp.sum(mlp_q * mlp_q)
    attn_q = attn_q.reshape(RB, 4, quarter).transpose(1, 0, 2)
    attn_s = in_order(core, attn_q, swap(attn_q, "c"), 2)
    mlp_s = (
        in_order(yl, mlp_q, swap(mlp_q, "yl"), 2)
        .reshape(2, RB, 4, half)
        .transpose(0, 2, 1, 3)
        .reshape(8, RB, half)
    )

    local_square = (
        grads_square
        + 0.25 * (jnp.sum(mod_s * mod_s) + jnp.sum(grad_temb * grad_temb))
        + jnp.sum(grad_table * grad_table)
        + jnp.sum(io_s * io_s)
        + jnp.sum(vec_s * vec_s)
    )
    sums = jnp.concatenate([local_square[None], loss_own[None], grad_hb])
    sums = jnp.pad(sums, (0, 128 - sums.shape[0]))
    sums = jnp.sum(to_all(sums[None], ALL), axis=0)[0]
    loss = sums[1] / count_all
    head_all = sums[2 : 2 + PATCH]
    grad_norm = jnp.sqrt(sums[0] + jnp.sum(head_all * head_all))
    factor = jnp.minimum(1.0, CLIP_NORM / (grad_norm + 1e-06))

    attn_moment = MOMENT_DECAY * attn_mom + factor * attn_s
    mlp_moment = MOMENT_DECAY * mlp_mom + factor * mlp_s
    mod_moment = MOMENT_DECAY * mod_mom + factor * mod_s
    temb_moment = MOMENT_DECAY * temb_mom + factor * grad_temb
    gram_attn = jnp.einsum("bij,bkj->bik", attn_moment, attn_moment, precision=HIGH)
    gram_mlp = jnp.einsum("bij,bkj->bik", mlp_moment, mlp_moment, precision=HIGH)
    gram_mod = jnp.einsum("bij,bkj->bik", mod_moment, mod_moment, precision=HIGH)
    temb_left, temb_right = temb_moment[:, :FREQ], temb_moment[:, FREQ:]
    gram_left = dot(temb_left, temb_left, 1, 1, HIGH)[None]
    gram_right = dot(temb_right, temb_right, 1, 1, HIGH)[None]
    gram_attn = gram_attn + swap(gram_attn, "yl")
    gram_mlp = gram_mlp + swap(gram_mlp, "c")
    maps = newton_maps(
        jnp.concatenate(
            [gram_attn, gram_left, gram_right, jnp.zeros((2, RB, RB), F32), gram_mlp, gram_mod]
        )
    )
    n_attn = 4 * RB
    attn_ortho = dot(
        maps[0, :n_attn, :n_attn], attn_moment.reshape(n_attn, half), 1, 0, HIGH
    ).reshape(attn_moment.shape)
    left_ortho = dot(
        maps[0, n_attn : n_attn + RB, n_attn : n_attn + RB], temb_left, 1, 0, HIGH
    )
    right_ortho = dot(
        maps[0, n_attn + RB : n_attn + 2 * RB, n_attn + RB : n_attn + 2 * RB],
        temb_right,
        1,
        0,
        HIGH,
    )
    mlp_ortho = dot(maps[1], mlp_moment.reshape(8 * RB, half), 1, 0, HIGH).reshape(
        mlp_moment.shape
    )
    mod_ortho = dot(maps[2], mod_moment.reshape(8 * RB, D), 1, 0, HIGH).reshape(mod_moment.shape)
    attn_new = attn_w - LR_MUON * attn_ortho
    mlp_new = mlp_w - LR_MUON * mlp_ortho
    mod_new = mod_w - LR_MUON * mod_ortho
    temb_new = temb_w - LR_MUON * jnp.concatenate([left_ortho, right_ortho], axis=1)
    table_new, table_first_new, table_second_new = adam(
        label_table, table_first, table_second, factor * grad_table, 0.3
    )
    io_rates = jnp.array([0.1, 0.01], F32).reshape(2, 1, 1)
    io_new, io_first_new, io_second_new = adam(io_w, io_first, io_second, factor * io_s, io_rates)
    vec_new, vec_first_new, vec_second_new = adam(
        vec_w, vec_first, vec_second, factor * vec_s, 0.05
    )
    headb_new, headb_first_new, headb_second_new = adam(
        head_b, headb_first, headb_second, factor * head_all, 0.05
    )
    return (
        loss,
        grad_norm,
        attn_new,
        attn_moment,
        attn_new.astype(BF),
        mlp_new,
        mlp_moment,
        mlp_new.astype(BF),
        mod_new,
        mod_moment,
        mod_new.astype(BF),
        temb_new,
        temb_moment,
        table_new,
        table_first_new,
        table_second_new,
        table_new.astype(BF),
        io_new,
        io_first_new,
        io_second_new,
        vec_new,
        vec_first_new,
        vec_second_new,
        headb_new,
        headb_first_new,
        headb_second_new,
    )


def chip_sum(halves):
    mine, other = halves
    return (mine.astype(F32) + swap(other, "c").astype(F32)).astype(BF)


def solution(mesh):
    fine = Mesh(mesh.devices.reshape(SHARD_SIZES + (2, 2)), ALL)
    lat = P(SHARD, None)
    one = P(SHARD)
    attn = P(None, SHARD, "yl")
    mlp = P(None, SHARD, "c")
    mod = P(None, SHARD, None)
    temb = P(SHARD, None)
    flat = P(None, ALL)
    io = P(None, None, ALL)
    rep = P()
    return jax.shard_map(
        on_device,
        mesh=fine,
        in_specs=(lat, lat, one, one, attn, attn, mlp, mlp, mod, mod, temb, temb)
        + (flat,) * 3
        + (io,) * 3
        + (flat,) * 3
        + (rep,) * 3,
        out_specs=(rep, rep)
        + (attn,) * 3
        + (mlp,) * 3
        + (mod,) * 3
        + (temb,) * 2
        + (flat,) * 4
        + (io,) * 3
        + (flat,) * 3
        + (rep,) * 3,
        check_vma=False,
    )
```
